768 devices in a mesh: row: 16 (over y_lo, x), col: 48 (over z, y_hi, core).
Axes of the slice: x: 4, y: 8 (y_hi: 2, y_lo: 4; y = y_hi * 4 + y_lo), z: 12, core: 2. Of those that a mesh axis runs over, the one named last changes fastest.
Arguments:
- transmission: float32 [2, 4096, 12288], P(None, 'row', 'col'), may hold values from -5 to 5
- probe_modes: float32 [2, 2, 256, 256], replicated, may hold values from -5 to 5
- measured: float32 [1536, 256, 256], P(('row', 'col')), may hold values from 0.2 to 8
- offset_down: int32 [1536], P(('row', 'col')), may hold values from 0 to 255, as said below
- offset_across: int32 [1536], P(('row', 'col')), may hold values from 0 to 255, as said below
Outputs:
- object_gradient: float32 [2, 4096, 12288], P(None, 'row', 'col')
- probe_gradient: float32 [2, 2, 256, 256], replicated
The draws below stay inside these ranges and needn't reach their ends.
Inputs may be any that keep to these rules, and one draw needn't show every extreme that they name: `offset_down`: offset of the scan's window start inside the tile of the device that holds the scan; a window reaches at most into the next tile down, the next tile across and the tile diagonally beyond. `offset_across`: as offset_down, along columns.
All inputs are finite; a program needn't handle non-finite values.
Results may differ from the reference program's by a relative error of at most 0.0001.
Values sent between devices are 32-bit elements; how exact they have to be, the bound alone decides.
A program may use at most 32 MiB of HBM per device.

```python
import math
import jax
import jax.numpy as jnp
from jax import lax

P_SIZE = 256
MODES = 2
TH = 256
TW = 256
SCAN_DEV = 2
NY = 4096
NX = 12288
SCANS = 1536
N_COL = 48


def draw_offset_down(key, part):
    values = jax.random.randint(jax.random.fold_in(key, 11), (SCANS,), 0, TH, dtype=jnp.int32)
    return values.at[0].set(TH - 1).at[1].set(0)


def draw_offset_across(key, part):
    values = jax.random.randint(jax.random.fold_in(key, 23), (SCANS,), 0, TW, dtype=jnp.int32)
    return values.at[1].set(TW - 1).at[0].set(0)


def levels(stream_key, dims, shards, low, high):
    gain, own = 1.0, jax.random.fold_in(stream_key, 6)
    for dim, blocks in shards:
        heights = jnp.exp(jax.random.uniform(jax.random.fold_in(own, dim), (blocks,), jnp.float32, low / len(shards), high / len(shards)))
        gain = gain * jnp.repeat(heights, dims[dim] // blocks).reshape([-1 if axis == dim else 1 for axis in range(len(dims))])
    return gain


def noise(key, dims, width, reach, cuts=(), kind=jnp.bfloat16):
    drawn = jax.random.normal(key, dims, jnp.float32) * width
    if len(cuts) > 0:
        drawn = levels(key, dims, cuts, -0.22, 0.18) * drawn
    return jnp.clip(drawn, min=-reach, max=reach).astype(kind)


def setup_inputs(seed: int = 0) -> dict:
    seeds = jax.random.split(jax.random.key(seed), 6)
    return {
        "transmission": noise(seeds[0], (2, NY, NX), 0.7, 5.0, ((1, 16), (2, 48)), jnp.float32),
        "probe_modes": noise(seeds[1], (MODES, 2, P_SIZE, P_SIZE), 0.7, 5.0, (), jnp.float32),
        "measured": jnp.clip(jnp.exp(math.log(8.0) - 3.6888794 * jax.random.uniform(seeds[2], (SCANS, P_SIZE, P_SIZE), jnp.float32) ** levels(seeds[2], (SCANS, P_SIZE, P_SIZE), ((0, 768),), -0.2, 0.2)), 0.2, 8.0),
        "offset_down": draw_offset_down(jax.random.fold_in(seeds[5], 71), 0),
        "offset_across": draw_offset_across(jax.random.fold_in(seeds[5], 71), 0),
    }


def reference(transmission, probe_modes, measured, offset_down, offset_across):
    padded = jnp.pad(transmission, ((0, 0), (0, P_SIZE), (0, P_SIZE)))
    modes = probe_modes[:, 0] + 1j * probe_modes[:, 1]

    def one_scan(which, carry):
        field, probe_total = carry
        device = which // SCAN_DEV
        top = (device // N_COL * TH + offset_down[which]).astype(jnp.int32)
        start_col = (device % N_COL * TW + offset_across[which]).astype(jnp.int32)
        zero = jnp.int32(0)
        window = lax.dynamic_slice(padded, (zero, top, start_col), (2, P_SIZE, P_SIZE))
        patch = window[0] + 1j * window[1]
        wave = jnp.fft.fft2(modes * patch[None], norm='ortho')
        resid = lax.optimization_barrier(jnp.sum(jnp.real(wave) ** 2 + jnp.imag(wave) ** 2, axis=0)) - measured[which]
        back = jnp.fft.ifft2(resid[None] * wave, norm='ortho')
        object_term = lax.optimization_barrier(jnp.sum(jnp.conj(modes) * back, axis=0))
        probe_term = jnp.conj(patch)[None] * back
        current = lax.dynamic_slice(field, (zero, top, start_col), (2, P_SIZE, P_SIZE))
        update = jnp.stack([jnp.real(object_term), jnp.imag(object_term)])
        field = lax.dynamic_update_slice(field, current + update, (zero, top, start_col))
        probe_total = probe_total + jnp.stack([jnp.real(probe_term), jnp.imag(probe_term)], axis=1)
        return (field, probe_total)
    start = (jnp.zeros_like(padded), jnp.zeros(probe_modes.shape, probe_modes.dtype))
    field, probe_total = lax.fori_loop(0, SCANS, one_scan, start)
    return (field[:, :NY, :NX], probe_total * (1.0 / math.sqrt(SCANS)))
```

```python
import functools
import math
import numpy as np
import jax
import jax.numpy as jnp
from jax import lax
from jax.experimental import pallas as pl
from jax.experimental.pallas import tpu as pltpu
from jax.sharding import PartitionSpec as P

F32, BF16 = jnp.float32, jnp.bfloat16


def split(v):
    high = v.astype(BF16)
    return high, (v - high.astype(F32)).astype(BF16)


def dft_tables(n):
    counter = np.arange(n)
    angles = (counter[:, None] * counter[None, :] % n) * (2.0 * math.pi / n)
    out = []
    for t in (np.cos(angles), np.sin(angles)):
        t = jnp.asarray((t / math.sqrt(n)).astype(np.float32))
        out += list(split(t))
    return jnp.stack(out)


def mm(a, b):
    return jnp.dot(a, b, preferred_element_type=F32)


def left(t, v):
    return mm(t[0], v[0]) + (mm(t[0], v[1]) + mm(t[1], v[0]))


def transform(c, s, re, im, sign):
    r, i = split(re), split(im)
    ar = left(c, r) - sign * left(s, i)
    ai = left(c, i) + sign * left(s, r)
    r, i = split(ar), split(ai)
    br = left(r, c) - sign * left(i, s)
    bi = left(i, c) + sign * left(r, s)
    return br, bi


def compute_kernel(down, across, region, probe, measured, tables, spread, probe_out, wave):
    n = probe.shape[-1]
    c = (tables[0], tables[1])
    s = (tables[2], tables[3])
    modes = probe.shape[0]
    scans = measured.shape[0]
    spread[...] = jnp.zeros_like(spread)
    for k in range(scans):
        y, x = down[k], across[k]
        over = lax.rem(y, 8)
        top = pl.multiple_of(y - over, 8)
        back_rows = lax.rem(n + 8 - over, n + 8)
        back_shift = lax.rem(2 * n - x, 2 * n)
        patch = []
        for part in range(2):
            rows = region[part, pl.ds(top, n + 8), :]
            rows = pltpu.roll(rows, back_rows, 0)[:n]
            patch.append(pltpu.roll(rows, back_shift, 1)[:, :n])
        pr, pi = patch
        total = -measured[k]
        for m in range(modes):
            mr, mi = probe[m, 0], probe[m, 1]
            wr, wi = transform(c, s, mr * pr - mi * pi, mr * pi + mi * pr, -1.0)
            wave[m, 0], wave[m, 1] = wr, wi
            total += wr * wr + wi * wi
        obj_r = obj_i = None
        for m in range(modes):
            br, bi = transform(c, s, total * wave[m, 0], total * wave[m, 1], 1.0)
            mr, mi = probe[m, 0], probe[m, 1]
            tr, ti = mr * br + mi * bi, mr * bi - mi * br
            obj_r = tr if m == 0 else obj_r + tr
            obj_i = ti if m == 0 else obj_i + ti
            qr, qi = pr * br + pi * bi, pr * bi - pi * br
            if k == 0:
                probe_out[m, 0], probe_out[m, 1] = qr, qi
            else:
                probe_out[m, 0] += qr
                probe_out[m, 1] += qi
        for part, g in enumerate((obj_r, obj_i)):
            wide = jnp.concatenate([g, jnp.zeros_like(g)], axis=1)
            wide = pltpu.roll(wide, x, 1)
            tall = jnp.concatenate([wide, jnp.zeros_like(wide[:8])], axis=0)
            spread[part, pl.ds(top, n + 8), :] += pltpu.roll(tall, over, 0)


def compute(down, across, region, probe, measured, tables):
    vm = pl.BlockSpec(memory_space=pltpu.VMEM)
    sm = pl.BlockSpec(memory_space=pltpu.SMEM)
    n = probe.shape[-1]
    return pl.pallas_call(
        compute_kernel,
        out_shape=[
            jax.ShapeDtypeStruct(region.shape, F32),
            jax.ShapeDtypeStruct(probe.shape, F32),
        ],
        in_specs=[sm, sm, vm, vm, vm, vm],
        out_specs=[vm, vm],
        scratch_shapes=[pltpu.VMEM((probe.shape[0], 2, n, n), F32)],
        compiler_params=pltpu.CompilerParams(vmem_limit_bytes=48 * 1024 * 1024),
    )(down, across, region, probe, measured, tables)


MESH = pl.DeviceIdType.MESH
NX_, NYL, NYH, NZ, NK = 4, 4, 2, 12, 2
NY_ = NYL * NYH


def place():
    r, c = lax.axis_index("row"), lax.axis_index("col")
    y = lax.rem(lax.div(c, NK), NYH) * NYL + lax.div(r, NX_)
    return lax.rem(r, NX_), y, lax.div(c, NK * NYH), lax.rem(c, NK)


def device(x, y, z, k):
    row = lax.rem(y, NYL) * NX_ + x
    return {"row": row, "col": z * (NK * NYH) + lax.div(y, NYL) * NK + k}


def up(i, d, n):
    return lax.rem(i + d, n)


def send(src, dst, ss, rs, to):
    copy = pltpu.make_async_remote_copy(
        src_ref=src, dst_ref=dst, send_sem=ss, recv_sem=rs, device_id=to, device_id_type=MESH
    )
    copy.start()
    return copy


def at(start, size):
    return pl.ds(pl.multiple_of(start, 16), size)


def total_kernel(scale, p, out, cin, acc, xin, ysum, yin, zin, cs, cr, xs, xr, ys, yr, zs, zr, gys, gyr, gxs, gxr, gcs, gcr):
    x, y, z, k = place()
    half = p.shape[0] // NK
    xb = half // NX_
    yb = xb // NY_
    other = 1 - k
    sibling = device(x, y, z, other)
    xpeer = [device(up(x, d, NX_), y, z, k) for d in range(1, NX_)]
    ypeer = [device(x, up(y, d, NY_), z, k) for d in range(1, NY_)]
    zpeer = [device(x, y, up(z, d, NZ), k) for d in range(1, NZ)]
    barrier = pltpu.get_barrier_semaphore()
    peers = [sibling] + xpeer + ypeer + zpeer
    for peer in peers:
        pl.semaphore_signal(barrier, inc=1, device_id=peer, device_id_type=MESH)
    pl.semaphore_wait(barrier, len(peers))
    sent = []
    order = [up(x, d, NX_) for d in range(1, NX_ + 1)]
    core = []
    for d, j in enumerate(order):
        core.append(send(p.at[at(other * half + j * xb, xb)], cin.at[at(j * xb, xb)], cs.at[d], cr.at[d], sibling))
    xc = []
    for d, j in enumerate(order):
        core[d].wait_recv()
        rows = at(j * xb, xb)
        acc[rows] = p[at(k * half + j * xb, xb)] + cin[rows]
        if d < NX_ - 1:
            xc.append(send(acc.at[rows], xin.at[d], xs.at[d], xr.at[d], xpeer[d]))
    for c in xc:
        c.wait_recv()
    yc = []
    for d in range(1, NY_ + 1):
        j = up(y, d, NY_)
        rows = at(j * yb, yb)
        v = acc[at(x * xb + j * yb, yb)]
        for i in range(NX_ - 1):
            v += xin[i, rows]
        ysum[rows] = v
        if d < NY_:
            yc.append(send(ysum.at[rows], yin.at[d - 1], ys.at[d - 1], yr.at[d - 1], ypeer[d - 1]))
    v = ysum[at(y * yb, yb)]
    for i, c in enumerate(yc):
        c.wait_recv()
        v += yin[i]
    zin[z] = v
    zc = [send(zin.at[z], zin.at[z], zs.at[d], zr.at[d], zpeer[d]) for d in range(NZ - 1)]
    for c in zc:
        c.wait_recv()
    v = zin[0]
    for i in range(1, NZ):
        v += zin[i]
    own = k * half + x * xb + y * yb
    out[at(own, yb)] = v * scale
    yg = [send(out.at[at(own, yb)], out.at[at(own, yb)], gys.at[d], gyr.at[d], ypeer[d]) for d in range(NY_ - 1)]
    xg = []
    cg = []

    def pass_on(e, rows):
        xg.append([send(out.at[rows], out.at[rows], gxs.at[e, d], gxr.at[e, d], xpeer[d]) for d in range(NX_ - 1)])

    def to_sibling(e, rows):
        cg.append(send(out.at[rows], out.at[rows], gcs.at[e], gcr.at[e], sibling))

    pass_on(0, at(own, yb))
    for e in range(1, NY_):
        yg[e - 1].wait_recv()
        pass_on(e, at(k * half + x * xb + up(y, NY_ - e, NY_) * yb, yb))
    to_sibling(0, at(k * half + x * xb, xb))
    for d in range(NX_ - 1):
        for e in range(NY_):
            xg[e][d].wait_recv()
        to_sibling(d + 1, at(k * half + up(x, NX_ - 1 - d, NX_) * xb, xb))
    for c in cg:
        c.wait_recv()
    for c in core + xc + yc + zc + yg + [c for g in xg for c in g] + cg:
        c.wait_send()


def total_over_devices(local, scale):
    rows = math.prod(local.shape[:-1])
    n = local.shape[-1]
    half = rows // NK
    xb = half // NX_
    yb = xb // NY_
    dma = pltpu.SemaphoreType.DMA
    pairs = [(NX_,), (NX_ - 1,), (NY_ - 1,), (NZ - 1,), (NY_ - 1,), (NY_, NX_ - 1), (NX_,)]
    vm = pl.BlockSpec(memory_space=pltpu.VMEM)
    out = pl.pallas_call(
        functools.partial(total_kernel, scale),
        out_shape=jax.ShapeDtypeStruct((rows, n), F32),
        in_specs=[vm],
        out_specs=vm,
        scratch_shapes=[
            pltpu.VMEM((half, n), F32),
            pltpu.VMEM((half, n), F32),
            pltpu.VMEM((NX_ - 1, xb, n), F32),
            pltpu.VMEM((xb, n), F32),
            pltpu.VMEM((NY_ - 1, yb, n), F32),
            pltpu.VMEM((NZ, yb, n), F32),
        ]
        + [dma(s) for s in pairs for _ in range(2)],
        compiler_params=pltpu.CompilerParams(collective_id=0, has_side_effects=True),
    )(local.reshape(rows, n))
    return out.reshape(local.shape)


def passed_along(block, axis, distance):
    devices = range(lax.axis_size(axis))
    route = [(i - distance, i) for i in devices if i - distance in devices]
    return lax.ppermute(block, axis, route)


def on_device(transmission, probe_modes, measured, offset_down, offset_across):
    n = probe_modes.shape[-1]
    right_strip = passed_along(transmission, "col", -1)
    upper_band = jnp.concatenate([transmission, right_strip], axis=2)
    lower_band = passed_along(upper_band, "row", -1)
    region = jnp.concatenate([upper_band, lower_band], axis=1)
    spread, local_probe = compute(
        offset_down, offset_across, region, probe_modes, measured, dft_tables(n)
    )
    scans = measured.shape[0] * lax.axis_size("row") * lax.axis_size("col")
    probe_gradient = total_over_devices(local_probe, 1.0 / math.sqrt(scans))
    from_above = passed_along(spread[:, n:, :], "row", 1)
    folded = spread[:, :n, :] + from_above
    from_left = passed_along(folded[:, :, n:], "col", 1)
    return (folded[:, :, :n] + from_left, probe_gradient)


def solution(mesh):
    in_specs = (
        P(None, "row", "col"),
        P(),
        P(("row", "col"), None, None),
        P(("row", "col")),
        P(("row", "col")),
    )
    out_specs = (P(None, "row", "col"), P())
    return jax.shard_map(
        on_device, mesh=mesh, in_specs=in_specs, out_specs=out_specs, check_vma=False
    )
```

```python
import functools
import math
import numpy as np
import jax
import jax.numpy as jnp
from jax import lax
from jax.experimental import pallas as pl
from jax.experimental.pallas import tpu as pltpu
from jax.sharding import PartitionSpec as P

F32, BF16 = jnp.float32, jnp.bfloat16


def split(v):
    high = v.astype(BF16)
    return high, (v - high.astype(F32)).astype(BF16)


def dft_tables(n):
    counter = np.arange(n)
    angles = (counter[:, None] * counter[None, :] % n) * (2.0 * math.pi / n)
    out = []
    for t in (np.cos(angles), np.sin(angles)):
        t = jnp.asarray((t / math.sqrt(n)).astype(np.float32))
        out += list(split(t))
    return jnp.stack(out)


def mm(a, b):
    return jnp.dot(a, b, preferred_element_type=F32)


def left(t, v):
    return mm(t[0], v[0]) + (mm(t[0], v[1]) + mm(t[1], v[0]))


def transform(c, s, re, im, sign):
    r, i = split(re), split(im)
    ar = left(c, r) - sign * left(s, i)
    ai = left(c, i) + sign * left(s, r)
    r, i = split(ar), split(ai)
    br = left(r, c) - sign * left(i, s)
    bi = left(i, c) + sign * left(r, s)
    return br, bi


def compute_kernel(down, across, region, probe, measured, tables, spread, probe_out, wave):
    n = probe.shape[-1]
    c = (tables[0], tables[1])
    s = (tables[2], tables[3])
    modes = probe.shape[0]
    scans = measured.shape[0]
    spread[...] = jnp.zeros_like(spread)
    for k in range(scans):
        y, x = down[k], across[k]
        over = lax.rem(y, 8)
        top = pl.multiple_of(y - over, 8)
        back_rows = lax.rem(n + 8 - over, n + 8)
        back_shift = lax.rem(2 * n - x, 2 * n)
        patch = []
        for part in range(2):
            rows = region[part, pl.ds(top, n + 8), :]
            rows = pltpu.roll(rows, back_rows, 0)[:n]
            patch.append(pltpu.roll(rows, back_shift, 1)[:, :n])
        pr, pi = patch
        total = -measured[k]
        for m in range(modes):
            mr, mi = probe[m, 0], probe[m, 1]
            wr, wi = transform(c, s, mr * pr - mi * pi, mr * pi + mi * pr, -1.0)
            wave[m, 0], wave[m, 1] = wr, wi
            total += wr * wr + wi * wi
        obj_r = obj_i = None
        for m in range(modes):
            br, bi = transform(c, s, total * wave[m, 0], total * wave[m, 1], 1.0)
            mr, mi = probe[m, 0], probe[m, 1]
            tr, ti = mr * br + mi * bi, mr * bi - mi * br
            obj_r = tr if m == 0 else obj_r + tr
            obj_i = ti if m == 0 else obj_i + ti
            qr, qi = pr * br + pi * bi, pr * bi - pi * br
            if k == 0:
                probe_out[m, 0], probe_out[m, 1] = qr, qi
            else:
                probe_out[m, 0] += qr
                probe_out[m, 1] += qi
        for part, g in enumerate((obj_r, obj_i)):
            wide = jnp.concatenate([g, jnp.zeros_like(g)], axis=1)
            wide = pltpu.roll(wide, x, 1)
            tall = jnp.concatenate([wide, jnp.zeros_like(wide[:8])], axis=0)
            spread[part, pl.ds(top, n + 8), :] += pltpu.roll(tall, over, 0)


def compute(down, across, region, probe, measured, tables):
    vm = pl.BlockSpec(memory_space=pltpu.VMEM)
    sm = pl.BlockSpec(memory_space=pltpu.SMEM)
    n = probe.shape[-1]
    return pl.pallas_call(
        compute_kernel,
        out_shape=[
            jax.ShapeDtypeStruct(region.shape, F32),
            jax.ShapeDtypeStruct(probe.shape, F32),
        ],
        in_specs=[sm, sm, vm, vm, vm, vm],
        out_specs=[vm, vm],
        scratch_shapes=[pltpu.VMEM((probe.shape[0], 2, n, n), F32)],
        compiler_params=pltpu.CompilerParams(vmem_limit_bytes=48 * 1024 * 1024),
    )(down, across, region, probe, measured, tables)


MESH = pl.DeviceIdType.MESH
NX_, NYL, NYH, NZ, NK = 4, 4, 2, 12, 2
NY_ = NYL * NYH


def place():
    r, c = lax.axis_index("row"), lax.axis_index("col")
    y = lax.rem(lax.div(c, NK), NYH) * NYL + lax.div(r, NX_)
    return lax.rem(r, NX_), y, lax.div(c, NK * NYH), lax.rem(c, NK)


def device(x, y, z, k):
    row = lax.rem(y, NYL) * NX_ + x
    return {"row": row, "col": z * (NK * NYH) + lax.div(y, NYL) * NK + k}


def up(i, d, n):
    return lax.rem(i + d, n)


def send(src, dst, ss, rs, to):
    copy = copy_to(src, dst, ss, rs, to)
    copy.start()
    return copy


def at(start, size):
    return pl.ds(pl.multiple_of(start, 16), size)


def gradients_kernel(scale, spread, p, tile, out, left_in, above_in, side_in, corner_in, under_sum, right_sum, cin, acc, xin, ysum, yin, zin,
                     ls, lr, as_, ar, ss, sr, ks, kr, cs, cr, xs, xr, ys, yr, zs, zr, gys, gyr, gxs, gxr, gcs, gcr):
    n = spread.shape[-1] // 2
    r, c = lax.axis_index("row"), lax.axis_index("col")
    last_row = NX_ * NYL - 1
    x, y, z, k = place()
    half = p.shape[0] // NK
    xb = half // NX_
    yb = xb // NY_
    other = 1 - k
    sibling = device(x, y, z, other)
    xpeer = [device(up(x, d, NX_), y, z, k) for d in range(1, NX_)]
    ypeer = [device(x, up(y, d, NY_), z, k) for d in range(1, NY_)]
    zpeer = [device(x, y, up(z, d, NZ), k) for d in range(1, NZ)]
    above, below, leftward, rightward = neighbours()
    greet([sibling, above, below, leftward, rightward] + xpeer + ypeer + zpeer)

    lo, hi = pl.ds(0, n), pl.ds(n, n)
    side_right = copy_to(spread.at[:, lo, hi], left_in, ls.at[0], lr.at[0], sibling)
    side_under = copy_to(spread.at[:, hi, hi], side_in, ss, sr, sibling)
    under0 = copy_to(spread.at[:, hi, lo], above_in, as_, ar, below)
    under1 = copy_to(under_sum, above_in, as_, ar, below)
    corners, rights, firsts = [], [], []
    for i, (q, h, s) in enumerate(pieces(n)):
        corners.append(copy_to(spread.at[q, pl.ds(n + h, s), hi], corner_in.at[q, pl.ds(h, s)], ks.at[i], kr.at[i], below))
        rights.append(copy_to(right_sum.at[q, pl.ds(h, s)], left_in.at[q, pl.ds(h, s)], ls.at[i], lr.at[i], rightward))
        firsts.append(copy_to(spread.at[q, pl.ds(h, s), hi], left_in.at[q, pl.ds(h, s)], ls.at[i], lr.at[i], rightward))

    order = [up(x, d, NX_) for d in range(1, NX_ + 1)]
    core = []
    for d, j in enumerate(order):
        core.append(send(p.at[at(other * half + j * xb, xb)], cin.at[at(j * xb, xb)], cs.at[d], cr.at[d], sibling))

    @pl.when(k == 0)
    def _():
        side_under.start()
        side_right.start()

    @pl.when((k == 1) & (r < last_row))
    def _():
        for copy in corners:
            copy.start()

    @pl.when((k == 1) & (r == 0))
    def _():
        for copy in firsts:
            copy.start()

    xc = []
    for d, j in enumerate(order):
        core[d].wait_recv()
        rows = at(j * xb, xb)
        acc[rows] = p[at(k * half + j * xb, xb)] + cin[rows]
        if d < NX_ - 1:
            xc.append(send(acc.at[rows], xin.at[d], xs.at[d], xr.at[d], xpeer[d]))

    @pl.when((k == 0) & (r < last_row))
    def _():
        under0.start()

    @pl.when(k == 1)
    def _():
        side_under.wait_recv()

        @pl.when(r < last_row)
        def _():
            under_sum[...] = spread[:, n:, :n] + side_in[...]
            under1.start()

    for copy in xc:
        copy.wait_recv()
    yc = []
    for d in range(1, NY_ + 1):
        j = up(y, d, NY_)
        rows = at(j * yb, yb)
        v = acc[at(x * xb + j * yb, yb)]
        for i in range(NX_ - 1):
            v += xin[i, rows]
        ysum[rows] = v
        if d < NY_:
            yc.append(send(ysum.at[rows], yin.at[d - 1], ys.at[d - 1], yr.at[d - 1], ypeer[d - 1]))

    @pl.when((k == 1) & (r > 0))
    def _():
        for i, (q, h, s) in enumerate(pieces(n)):
            corners[i].wait_recv()
            right_sum[q, h : h + s] = spread[q, h : h + s, n:] + corner_in[q, h : h + s]
            rights[i].start()

    v = ysum[at(y * yb, yb)]
    for i, copy in enumerate(yc):
        copy.wait_recv()
        v += yin[i]
    zin[z] = v
    zc = [send(zin.at[z], zin.at[z], zs.at[d], zr.at[d], zpeer[d]) for d in range(NZ - 1)]
    for copy in zc:
        copy.wait_recv()
    v = zin[0]
    for i in range(1, NZ):
        v += zin[i]
    own = k * half + x * xb + y * yb
    out[at(own, yb)] = v * scale
    yg = [send(out.at[at(own, yb)], out.at[at(own, yb)], gys.at[d], gyr.at[d], ypeer[d]) for d in range(NY_ - 1)]
    xg = []
    cg = []

    def pass_on(e, rows):
        xg.append([send(out.at[rows], out.at[rows], gxs.at[e, d], gxr.at[e, d], xpeer[d]) for d in range(NX_ - 1)])

    def to_sibling(e, rows):
        cg.append(send(out.at[rows], out.at[rows], gcs.at[e], gcr.at[e], sibling))

    pass_on(0, at(own, yb))
    for e in range(1, NY_):
        yg[e - 1].wait_recv()
        pass_on(e, at(k * half + x * xb + up(y, NY_ - e, NY_) * yb, yb))
    to_sibling(0, at(k * half + x * xb, xb))

    @pl.when(r > 0)
    def _():
        under0.wait_recv()
        tile[...] = spread[:, :n, :n] + above_in[...]

    @pl.when(r == 0)
    def _():
        tile[...] = spread[:, :n, :n]

    @pl.when(k == 1)
    def _():
        side_right.wait_recv()

    @pl.when(k == 0)
    def _():
        for copy in rights:
            copy.wait_recv()

    @pl.when(c > 0)
    def _():
        tile[...] += left_in[...]

    for d in range(NX_ - 1):
        for e in range(NY_):
            xg[e][d].wait_recv()
        to_sibling(d + 1, at(k * half + up(x, NX_ - 1 - d, NX_) * xb, xb))
    for copy in cg:
        copy.wait_recv()
    for copy in core + xc + yc + zc + yg + [v for g in xg for v in g] + cg:
        copy.wait_send()

    @pl.when(k == 0)
    def _():
        side_under.wait_send()
        side_right.wait_send()

    @pl.when(k == 1)
    def _():
        for copy in rights:
            copy.wait_send()

    @pl.when(r < last_row)
    def _():
        under0.wait_send()

        @pl.when(k == 1)
        def _():
            for copy in corners:
                copy.wait_send()


def gradients(spread, local, scale):
    rows = math.prod(local.shape[:-1])
    n = local.shape[-1]
    half = rows // NK
    xb = half // NX_
    yb = xb // NY_
    dma = pltpu.SemaphoreType.DMA
    pairs = [(4,), (), (), (4,), (NX_,), (NX_ - 1,), (NY_ - 1,), (NZ - 1,), (NY_ - 1,), (NY_, NX_ - 1), (NX_,)]
    vm = pl.BlockSpec(memory_space=pltpu.VMEM)
    block = pltpu.VMEM((2, n, n), F32)
    tile, out = pl.pallas_call(
        functools.partial(gradients_kernel, scale),
        out_shape=[jax.ShapeDtypeStruct((2, n, n), F32), jax.ShapeDtypeStruct((rows, n), F32)],
        in_specs=[vm, vm],
        out_specs=[vm, vm],
        scratch_shapes=[block] * 6
        + [
            pltpu.VMEM((half, n), F32),
            pltpu.VMEM((half, n), F32),
            pltpu.VMEM((NX_ - 1, xb, n), F32),
            pltpu.VMEM((xb, n), F32),
            pltpu.VMEM((NY_ - 1, yb, n), F32),
            pltpu.VMEM((NZ, yb, n), F32),
        ]
        + [dma(s) for s in pairs for _ in range(2)],
        compiler_params=pltpu.CompilerParams(
            collective_id=0, has_side_effects=True, vmem_limit_bytes=48 * 1024 * 1024
        ),
    )(spread, local.reshape(rows, n))
    return tile, out.reshape(local.shape)


def neighbours():
    r, c = lax.axis_index("row"), lax.axis_index("col")
    rows, cols = NX_ * NYL, NZ * NYH * NK
    above = {"row": lax.rem(r + rows - 1, rows), "col": c}
    below = {"row": lax.rem(r + 1, rows), "col": c}
    leftward = {"row": r, "col": lax.rem(c + cols - 1, cols)}
    rightward = {"row": r, "col": lax.rem(c + 1, cols)}
    return above, below, leftward, rightward


def greet(peers):
    barrier = pltpu.get_barrier_semaphore()
    for peer in peers:
        pl.semaphore_signal(barrier, inc=1, device_id=peer, device_id_type=MESH)
    pl.semaphore_wait(barrier, len(peers))


def copy_to(src, dst, ss, rs, to):
    return pltpu.make_async_remote_copy(
        src_ref=src, dst_ref=dst, send_sem=ss, recv_sem=rs, device_id=to, device_id_type=MESH
    )


def pieces(n):
    return [(part, h * (n // 2), n // 2) for part in range(2) for h in range(2)]


def gather_kernel(t, region, rs_, rr, bs, br, ds, dr):
    n = t.shape[-1]
    r, c = lax.axis_index("row"), lax.axis_index("col")
    last_row, last_col = NX_ * NYL - 1, NZ * NYH * NK - 1
    k = lax.rem(c, NK)
    above, below, leftward, rightward = neighbours()
    greet([above, below, leftward, rightward])
    left_part = pl.ds(0, n)
    right_part = pl.ds(n, n)
    to_left, to_above, on_above, on_sibling = [], [], [], []
    for i, (p, h, s) in enumerate(pieces(n)):
        own = t.at[p, pl.ds(h, s)]
        right = region.at[p, pl.ds(h, s), right_part]
        under = region.at[p, pl.ds(n + h, s), left_part]
        corner = region.at[p, pl.ds(n + h, s), right_part]
        to_left.append(copy_to(own, right, rs_.at[i], rr.at[i], leftward))
        to_above.append(copy_to(own, under, bs.at[i], br.at[i], above))
        on_above.append(copy_to(right, corner, ds.at[i], dr.at[i], above))
        on_sibling.append(copy_to(under, corner, ds.at[i], dr.at[i], leftward))
    for i in range(len(to_left)):
        to_left[i].start()
        pl.when(r > 0)(to_above[i].start)
    region[:, :n, :n] = t[...]

    @pl.when(r == last_row)
    def _():
        region[:, n:, :] = jnp.zeros((2, n, 2 * n), F32)

    @pl.when(k == 1)
    def _():
        for i in range(len(to_left)):
            @pl.when(r < last_row)
            def _():
                to_above[i].wait_recv()
                on_sibling[i].start()

            to_left[i].wait_recv()

            @pl.when(r > 0)
            def _():
                on_above[i].start()

        for i in range(len(to_left)):
            @pl.when(r < last_row)
            def _():
                on_above[i].wait_recv()
                on_sibling[i].wait_send()

            @pl.when(r > 0)
            def _():
                on_above[i].wait_send()

    @pl.when(k == 0)
    def _():
        for i in range(len(to_left)):
            to_left[i].wait_recv()

            @pl.when(r < last_row)
            def _():
                to_above[i].wait_recv()
                on_sibling[i].wait_recv()

    for i in range(len(to_left)):
        to_left[i].wait_send()
        pl.when(r > 0)(to_above[i].wait_send)

    @pl.when(c == last_col)
    def _():
        region[:, :, n:] = jnp.zeros((2, 2 * n, n), F32)


def gather_region(tile):
    n = tile.shape[-1]
    vm = pl.BlockSpec(memory_space=pltpu.VMEM)
    return pl.pallas_call(
        gather_kernel,
        out_shape=jax.ShapeDtypeStruct((2, 2 * n, 2 * n), F32),
        in_specs=[vm],
        out_specs=vm,
        scratch_shapes=[pltpu.SemaphoreType.DMA((4,))] * 6,
        compiler_params=pltpu.CompilerParams(collective_id=1, has_side_effects=True),
    )(tile)


def on_device(transmission, probe_modes, measured, offset_down, offset_across):
    region = gather_region(transmission)
    spread, local_probe = compute(
        offset_down, offset_across, region, probe_modes, measured, dft_tables(probe_modes.shape[-1])
    )
    scans = measured.shape[0] * lax.axis_size("row") * lax.axis_size("col")
    return gradients(spread, local_probe, 1.0 / math.sqrt(scans))


def solution(mesh):
    in_specs = (
        P(None, "row", "col"),
        P(),
        P(("row", "col"), None, None),
        P(("row", "col")),
        P(("row", "col")),
    )
    out_specs = (P(None, "row", "col"), P())
    return jax.shard_map(
        on_device, mesh=mesh, in_specs=in_specs, out_specs=out_specs, check_vma=False
    )
```

```python
import functools
import math
import numpy as np
import jax
import jax.numpy as jnp
from jax import lax
from jax.experimental import pallas as pl
from jax.experimental.pallas import tpu as pltpu
from jax.sharding import PartitionSpec as P

F32, BF16 = jnp.float32, jnp.bfloat16


def split(v):
    high = v.astype(BF16)
    return high, (v - high.astype(F32)).astype(BF16)


def dft_tables(n):
    counter = np.arange(n)
    angles = (counter[:, None] * counter[None, :] % n) * (2.0 * math.pi / n)
    out = []
    for t in (np.cos(angles), np.sin(angles)):
        t = jnp.asarray((t / math.sqrt(n)).astype(np.float32))
        out += list(split(t))
    return jnp.stack(out)


def mm(a, b):
    return jnp.dot(a, b, preferred_element_type=F32)


def left(t, v):
    return mm(t[0], v[0]) + (mm(t[0], v[1]) + mm(t[1], v[0]))


def transform(c, s, re, im, sign):
    r, i = split(re), split(im)
    ar = left(c, r) - sign * left(s, i)
    ai = left(c, i) + sign * left(s, r)
    r, i = split(ar), split(ai)
    br = left(r, c) - sign * left(i, s)
    bi = left(i, c) + sign * left(r, s)
    return br, bi


def compute_kernel(down, across, region, probe, measured, tables, spread, probe_out, wave):
    n = probe.shape[-1]
    c = (tables[0], tables[1])
    s = (tables[2], tables[3])
    modes = probe.shape[0]
    scans = measured.shape[0]
    spread[...] = jnp.zeros_like(spread)
    for k in range(scans):
        y, x = down[k], across[k]
        over = lax.rem(y, 8)
        top = pl.multiple_of(y - over, 8)
        back_rows = lax.rem(n + 8 - over, n + 8)
        back_shift = lax.rem(2 * n - x, 2 * n)
        patch = []
        for part in range(2):
            rows = region[part, pl.ds(top, n + 8), :]
            rows = pltpu.roll(rows, back_rows, 0)[:n]
            patch.append(pltpu.roll(rows, back_shift, 1)[:, :n])
        pr, pi = patch
        total = -measured[k]
        for m in range(modes):
            mr, mi = probe[m, 0], probe[m, 1]
            wr, wi = transform(c, s, mr * pr - mi * pi, mr * pi + mi * pr, -1.0)
            wave[m, 0], wave[m, 1] = wr, wi
            total += wr * wr + wi * wi
        obj_r = obj_i = None
        for m in range(modes):
            br, bi = transform(c, s, total * wave[m, 0], total * wave[m, 1], 1.0)
            mr, mi = probe[m, 0], probe[m, 1]
            tr, ti = mr * br + mi * bi, mr * bi - mi * br
            obj_r = tr if m == 0 else obj_r + tr
            obj_i = ti if m == 0 else obj_i + ti
            qr, qi = pr * br + pi * bi, pr * bi - pi * br
            if k == 0:
                probe_out[m, 0], probe_out[m, 1] = qr, qi
            else:
                probe_out[m, 0] += qr
                probe_out[m, 1] += qi
        for part, g in enumerate((obj_r, obj_i)):
            wide = jnp.concatenate([g, jnp.zeros_like(g)], axis=1)
            wide = pltpu.roll(wide, x, 1)
            tall = jnp.concatenate([wide, jnp.zeros_like(wide[:8])], axis=0)
            spread[part, pl.ds(top, n + 8), :] += pltpu.roll(tall, over, 0)


def compute(down, across, region, probe, measured, tables):
    vm = pl.BlockSpec(memory_space=pltpu.VMEM)
    sm = pl.BlockSpec(memory_space=pltpu.SMEM)
    n = probe.shape[-1]
    return pl.pallas_call(
        compute_kernel,
        out_shape=[
            jax.ShapeDtypeStruct(region.shape, F32),
            jax.ShapeDtypeStruct(probe.shape, F32),
        ],
        in_specs=[sm, sm, vm, vm, vm, vm],
        out_specs=[vm, vm],
        scratch_shapes=[pltpu.VMEM((probe.shape[0], 2, n, n), F32)],
        compiler_params=pltpu.CompilerParams(vmem_limit_bytes=48 * 1024 * 1024),
    )(down, across, region, probe, measured, tables)


MESH = pl.DeviceIdType.MESH
NX_, NYL, NYH, NZ, NK = 4, 4, 2, 12, 2
NY_ = NYL * NYH


def place():
    r, c = lax.axis_index("row"), lax.axis_index("col")
    y = lax.rem(lax.div(c, NK), NYH) * NYL + lax.div(r, NX_)
    return lax.rem(r, NX_), y, lax.div(c, NK * NYH), lax.rem(c, NK)


def device(x, y, z, k):
    row = lax.rem(y, NYL) * NX_ + x
    return {"row": row, "col": z * (NK * NYH) + lax.div(y, NYL) * NK + k}


def up(i, d, n):
    return lax.rem(i + d, n)


def send(src, dst, ss, rs, to):
    copy = copy_to(src, dst, ss, rs, to)
    copy.start()
    return copy


def at(start, size):
    return pl.ds(pl.multiple_of(start, 16), size)


def gradients_kernel(scale, spread, p, tile, out, left_in, above_in, side_in, corner_in, under_sum, right_sum, via, cin, acc, xin, ysum, yin, zin,
                     ls, lr, as_, ar, ss, sr, ks, kr, cs, cr, xs, xr, ys, yr, zs, zr, gys, gyr, gxs, gxr, gcs, gcr, vr, fs):
    n = spread.shape[-1] // 2
    r, c = lax.axis_index("row"), lax.axis_index("col")
    last_row = NX_ * NYL - 1
    x, y, z, k = place()
    half = p.shape[0] // NK
    xb = half // NX_
    yb = xb // NY_
    other = 1 - k
    sibling = device(x, y, z, other)
    xpeer = [device(up(x, d, NX_), y, z, k) for d in range(1, NX_)]
    ypeer = [device(x, up(y, d, NY_), z, k) for d in range(1, NY_)]
    zpeer = [device(x, y, up(z, d, NZ), k) for d in range(1, NZ)]
    above, below, leftward, rightward = neighbours()
    y_lo = lax.div(r, NX_)
    detours = (x == NX_ - 1) & (r < last_row)
    passes = (x == 0) & (y_lo < NYL - 1)
    detour = {"row": lax.rem(r + NX_ * NYL - (NX_ - 1), NX_ * NYL), "col": c}
    onward = {"row": lax.rem(r + NX_, NX_ * NYL), "col": c}
    sources = [{"row": lax.rem(r + d, NX_ * NYL), "col": c} for d in (NX_ - 1, NX_ * NYL - NX_)]
    greet([sibling, above, below, leftward, rightward] + sources + xpeer + ypeer + zpeer)


    lo, hi = pl.ds(0, n), pl.ds(n, n)
    side_right = copy_to(spread.at[:, lo, hi], left_in, ls.at[0], lr.at[0], sibling)
    side_under = copy_to(spread.at[:, hi, hi], side_in, ss, sr, sibling)
    cut = pieces(n)
    middle = len(cut) // 2
    under, under_round, under_pass, corners, corner_round, corner_pass, rights, firsts = [[] for _ in range(8)]
    for i, (q, h, s) in enumerate(cut):
        rows = pl.ds(h, s)
        below_left, below_right = under_sum.at[q, rows], spread.at[q, pl.ds(n + h, s), hi]
        under.append(copy_to(below_left, above_in.at[q, rows], as_.at[i], ar.at[i], below))
        corners.append(copy_to(below_right, corner_in.at[q, rows], ks.at[i], kr.at[i], below))
        rights.append(copy_to(right_sum.at[q, rows], left_in.at[q, rows], ls.at[i], lr.at[i], rightward))
        firsts.append(copy_to(spread.at[q, rows, hi], left_in.at[q, rows], ls.at[i], lr.at[i], rightward))
        if i >= middle:
            e, f = i - middle, i
            under_round.append(copy_to(below_left, via.at[e], as_.at[i], vr.at[e], detour))
            corner_round.append(copy_to(below_right, via.at[f], ks.at[i], vr.at[f], detour))
            under_pass.append(copy_to(via.at[e], above_in.at[q, rows], fs.at[e], ar.at[i], onward))
            corner_pass.append(copy_to(via.at[f], corner_in.at[q, rows], fs.at[f], kr.at[i], onward))

    def downward(direct, rounds):
        for i in list(range(middle, len(cut))) + list(range(middle)):
            if i < middle:
                pl.when(r < last_row)(direct[i].start)
            else:
                pl.when((r < last_row) & (x < NX_ - 1))(direct[i].start)
                pl.when(detours)(rounds[i - middle].start)

    def pass_down(rounds, passing):
        @pl.when(passes)
        def _():
            for e in range(middle):
                rounds[e].wait_recv()
                passing[e].start()

    order = [up(x, d, NX_) for d in range(1, NX_ + 1)]
    core = []
    for d, j in enumerate(order):
        core.append(send(p.at[at(other * half + j * xb, xb)], cin.at[at(j * xb, xb)], cs.at[d], cr.at[d], sibling))

    @pl.when(k == 0)
    def _():
        side_under.start()
        side_right.start()

    @pl.when(k == 1)
    def _():
        downward(corners, corner_round)

    @pl.when((k == 1) & (r == 0))
    def _():
        for copy in firsts:
            copy.start()

    xc = []
    for d, j in enumerate(order):
        core[d].wait_recv()
        rows = at(j * xb, xb)
        acc[rows] = p[at(k * half + j * xb, xb)] + cin[rows]
        if d < NX_ - 1:
            xc.append(send(acc.at[rows], xin.at[d], xs.at[d], xr.at[d], xpeer[d]))

    @pl.when(k == 0)
    def _():
        under_sum[...] = spread[:, n:, :n]

    @pl.when(k == 1)
    def _():
        side_under.wait_recv()
        under_sum[...] = spread[:, n:, :n] + side_in[...]

    for copy in xc:
        copy.wait_recv()
    yc = []
    for d in range(1, NY_ + 1):
        j = up(y, d, NY_)
        rows = at(j * yb, yb)
        v = acc[at(x * xb + j * yb, yb)]
        for i in range(NX_ - 1):
            v += xin[i, rows]
        ysum[rows] = v
        if d < NY_:
            yc.append(send(ysum.at[rows], yin.at[d - 1], ys.at[d - 1], yr.at[d - 1], ypeer[d - 1]))

    downward(under, under_round)

    @pl.when(k == 1)
    def _():
        pass_down(corner_round, corner_pass)

    @pl.when((k == 1) & (r > 0))
    def _():
        for i, (q, h, s) in enumerate(cut):
            corners[i].wait_recv()
            right_sum[q, h : h + s] = spread[q, h : h + s, n:] + corner_in[q, h : h + s]
            rights[i].start()

    v = ysum[at(y * yb, yb)]
    for i, copy in enumerate(yc):
        copy.wait_recv()
        v += yin[i]
    zin[z] = v
    zc = [send(zin.at[z], zin.at[z], zs.at[d], zr.at[d], zpeer[d]) for d in range(NZ - 1)]
    pass_down(under_round, under_pass)
    for copy in zc:
        copy.wait_recv()
    v = zin[0]
    for i in range(1, NZ):
        v += zin[i]
    own = k * half + x * xb + y * yb
    out[at(own, yb)] = v * scale
    yg = [send(out.at[at(own, yb)], out.at[at(own, yb)], gys.at[d], gyr.at[d], ypeer[d]) for d in range(NY_ - 1)]
    xg = []
    cg = []

    def pass_on(e, rows):
        xg.append([send(out.at[rows], out.at[rows], gxs.at[e, d], gxr.at[e, d], xpeer[d]) for d in range(NX_ - 1)])

    def to_sibling(e, rows):
        cg.append(send(out.at[rows], out.at[rows], gcs.at[e], gcr.at[e], sibling))

    pass_on(0, at(own, yb))
    for e in range(1, NY_):
        yg[e - 1].wait_recv()
        pass_on(e, at(k * half + x * xb + up(y, NY_ - e, NY_) * yb, yb))
    to_sibling(0, at(k * half + x * xb, xb))

    @pl.when(r > 0)
    def _():
        for copy in under:
            copy.wait_recv()
        tile[...] = spread[:, :n, :n] + above_in[...]

    @pl.when(r == 0)
    def _():
        tile[...] = spread[:, :n, :n]

    @pl.when(k == 1)
    def _():
        side_right.wait_recv()

    @pl.when(k == 0)
    def _():
        for copy in rights:
            copy.wait_recv()

    @pl.when(c > 0)
    def _():
        tile[...] += left_in[...]

    for d in range(NX_ - 1):
        for e in range(NY_):
            xg[e][d].wait_recv()
        to_sibling(d + 1, at(k * half + up(x, NX_ - 1 - d, NX_) * xb, xb))
    for copy in cg:
        copy.wait_recv()
    for copy in core + xc + yc + zc + yg + [v for g in xg for v in g] + cg:
        copy.wait_send()

    @pl.when(k == 0)
    def _():
        side_under.wait_send()
        side_right.wait_send()

    @pl.when(k == 1)
    def _():
        for copy in rights:
            copy.wait_send()

    @pl.when(passes)
    def _():
        for copy in under_pass:
            copy.wait_send()

        @pl.when(k == 1)
        def _():
            for copy in corner_pass:
                copy.wait_send()

    @pl.when(r < last_row)
    def _():
        for copy in under:
            copy.wait_send()

        @pl.when(k == 1)
        def _():
            for copy in corners:
                copy.wait_send()


def gradients(spread, local, scale):
    rows = math.prod(local.shape[:-1])
    n = local.shape[-1]
    half = rows // NK
    xb = half // NX_
    yb = xb // NY_
    dma = pltpu.SemaphoreType.DMA
    pairs = [(4,), (4,), (), (4,), (NX_,), (NX_ - 1,), (NY_ - 1,), (NZ - 1,), (NY_ - 1,), (NY_, NX_ - 1), (NX_,), (4,)]
    vm = pl.BlockSpec(memory_space=pltpu.VMEM)
    block = pltpu.VMEM((2, n, n), F32)
    tile, out = pl.pallas_call(
        functools.partial(gradients_kernel, scale),
        out_shape=[jax.ShapeDtypeStruct((2, n, n), F32), jax.ShapeDtypeStruct((rows, n), F32)],
        in_specs=[vm, vm],
        out_specs=[vm, vm],
        scratch_shapes=[block] * 6
        + [
            pltpu.VMEM((4, n // 2, n), F32),
            pltpu.VMEM((half, n), F32),
            pltpu.VMEM((half, n), F32),
            pltpu.VMEM((NX_ - 1, xb, n), F32),
            pltpu.VMEM((xb, n), F32),
            pltpu.VMEM((NY_ - 1, yb, n), F32),
            pltpu.VMEM((NZ, yb, n), F32),
        ]
        + [dma(s) for s in pairs for _ in range(2)],
        compiler_params=pltpu.CompilerParams(
            collective_id=0, has_side_effects=True, vmem_limit_bytes=48 * 1024 * 1024
        ),
    )(spread, local.reshape(rows, n))
    return tile, out.reshape(local.shape)


def neighbours():
    r, c = lax.axis_index("row"), lax.axis_index("col")
    rows, cols = NX_ * NYL, NZ * NYH * NK
    above = {"row": lax.rem(r + rows - 1, rows), "col": c}
    below = {"row": lax.rem(r + 1, rows), "col": c}
    leftward = {"row": r, "col": lax.rem(c + cols - 1, cols)}
    rightward = {"row": r, "col": lax.rem(c + 1, cols)}
    return above, below, leftward, rightward


def greet(peers):
    barrier = pltpu.get_barrier_semaphore()
    for peer in peers:
        pl.semaphore_signal(barrier, inc=1, device_id=peer, device_id_type=MESH)
    pl.semaphore_wait(barrier, len(peers))


def copy_to(src, dst, ss, rs, to):
    return pltpu.make_async_remote_copy(
        src_ref=src, dst_ref=dst, send_sem=ss, recv_sem=rs, device_id=to, device_id_type=MESH
    )


def pieces(n):
    return [(part, h * (n // 2), n // 2) for part in range(2) for h in range(2)]


def gather_kernel(t, region, via, rs_, rr, bs, br, ds, dr, vr, fs):
    n = t.shape[-1]
    r, c = lax.axis_index("row"), lax.axis_index("col")
    last_row, last_col = NX_ * NYL - 1, NZ * NYH * NK - 1
    k, x, y_lo = lax.rem(c, NK), lax.rem(r, NX_), lax.div(r, NX_)
    above, below, leftward, rightward = neighbours()
    detours = (x == 0) & (r > 0)
    passes = (x == NX_ - 1) & (y_lo > 0)
    detour = {"row": lax.rem(r + NX_ - 1, NX_ * NYL), "col": c}
    onward = {"row": lax.rem(r + NX_ * NYL - NX_, NX_ * NYL), "col": c}
    sources = [{"row": lax.rem(r + d, NX_ * NYL), "col": c} for d in (NX_ * NYL - NX_ + 1, NX_)]
    greet([above, below, leftward, rightward] + sources)

    left_part = pl.ds(0, n)
    right_part = pl.ds(n, n)
    cut = pieces(n)
    half = len(cut) // 2
    to_left, to_above, on_above, on_sibling = [], [], [], []
    round_above, round_on, pass_above, pass_on = [], [], [], []
    for i, (p, h, s) in enumerate(cut):
        own = t.at[p, pl.ds(h, s)]
        right = region.at[p, pl.ds(h, s), right_part]
        under = region.at[p, pl.ds(n + h, s), left_part]
        corner = region.at[p, pl.ds(n + h, s), right_part]
        to_left.append(copy_to(own, right, rs_.at[i], rr.at[i], leftward))
        to_above.append(copy_to(own, under, bs.at[i], br.at[i], above))
        on_above.append(copy_to(right, corner, ds.at[i], dr.at[i], above))
        on_sibling.append(copy_to(under, corner, ds.at[i], dr.at[i], leftward))
        if i >= half:
            a, b = i - half, i
            round_above.append(copy_to(own, via.at[a], bs.at[i], vr.at[a], detour))
            round_on.append(copy_to(right, via.at[b], ds.at[i], vr.at[b], detour))
            pass_above.append(copy_to(via.at[a], under, fs.at[a], br.at[i], onward))
            pass_on.append(copy_to(via.at[b], corner, fs.at[b], dr.at[i], onward))

    def upward(direct, rounds, i):
        if i < half:
            pl.when(r > 0)(direct[i].start)
        else:
            pl.when((r > 0) & (x > 0))(direct[i].start)
            pl.when(detours)(rounds[i - half].start)

    for i in range(len(cut)):
        to_left[i].start()
    for i in range(len(cut)):
        upward(to_above, round_above, i)
    region[:, :n, :n] = t[...]

    @pl.when(r == last_row)
    def _():
        region[:, n:, :] = jnp.zeros((2, n, 2 * n), F32)

    def pass_first():
        for a in range(half):
            round_above[a].wait_recv()
            pass_above[a].start()

    @pl.when(k == 1)
    def _():
        for i in range(len(cut)):
            @pl.when(r < last_row)
            def _():
                to_above[i].wait_recv()
                on_sibling[i].start()

            to_left[i].wait_recv()
            upward(on_above, round_on, i)
            if i == half - 1:
                pl.when(passes)(pass_first)

        @pl.when(passes)
        def _():
            for a in range(half):
                round_on[a].wait_recv()
                pass_on[a].start()

        for i in range(len(cut)):
            @pl.when(r < last_row)
            def _():
                on_above[i].wait_recv()
                on_sibling[i].wait_send()

            @pl.when(r > 0)
            def _():
                on_above[i].wait_send()

        @pl.when(passes)
        def _():
            for a in range(half):
                pass_on[a].wait_send()

    @pl.when(k == 0)
    def _():
        pl.when(passes)(pass_first)
        for i in range(len(cut)):
            to_left[i].wait_recv()

            @pl.when(r < last_row)
            def _():
                to_above[i].wait_recv()
                on_sibling[i].wait_recv()

    for i in range(len(cut)):
        to_left[i].wait_send()
        pl.when(r > 0)(to_above[i].wait_send)

    @pl.when(passes)
    def _():
        for a in range(half):
            pass_above[a].wait_send()

    @pl.when(c == last_col)
    def _():
        region[:, :, n:] = jnp.zeros((2, 2 * n, n), F32)


def gather_region(tile):
    n = tile.shape[-1]
    vm = pl.BlockSpec(memory_space=pltpu.VMEM)
    return pl.pallas_call(
        gather_kernel,
        out_shape=jax.ShapeDtypeStruct((2, 2 * n, 2 * n), F32),
        in_specs=[vm],
        out_specs=vm,
        scratch_shapes=[pltpu.VMEM((4, n // 2, n), F32)] + [pltpu.SemaphoreType.DMA((4,))] * 8,
        compiler_params=pltpu.CompilerParams(collective_id=1, has_side_effects=True),
    )(tile)


def on_device(transmission, probe_modes, measured, offset_down, offset_across):
    region = gather_region(transmission)
    spread, local_probe = compute(
        offset_down, offset_across, region, probe_modes, measured, dft_tables(probe_modes.shape[-1])
    )
    scans = measured.shape[0] * lax.axis_size("row") * lax.axis_size("col")
    return gradients(spread, local_probe, 1.0 / math.sqrt(scans))


def solution(mesh):
    in_specs = (
        P(None, "row", "col"),
        P(),
        P(("row", "col"), None, None),
        P(("row", "col")),
        P(("row", "col")),
    )
    out_specs = (P(None, "row", "col"), P())
    return jax.shard_map(
        on_device, mesh=mesh, in_specs=in_specs, out_specs=out_specs, check_vma=False
    )
```

```python
import functools
import math
import numpy as np
import jax
import jax.numpy as jnp
from jax import lax
from jax.experimental import pallas as pl
from jax.experimental.pallas import tpu as pltpu
from jax.sharding import PartitionSpec as P

F32, BF16 = jnp.float32, jnp.bfloat16


def split(v):
    high = v.astype(BF16)
    return high, (v - high.astype(F32)).astype(BF16)


def dft_tables(n):
    counter = np.arange(n)
    angles = (counter[:, None] * counter[None, :] % n) * (2.0 * math.pi / n)
    out = []
    for t in (np.cos(angles), np.sin(angles)):
        t = jnp.asarray((t / math.sqrt(n)).astype(np.float32))
        out += list(split(t))
    return jnp.stack(out)


def mm(a, b):
    return jnp.dot(a, b, preferred_element_type=F32)


def transform(c, s, pairs, sign):
    ch, cl = c
    sh, sl = s
    tc = [ch, ch, cl]
    ts = [sh, sh, sl]
    neg = [-sh, -sh, -sl]
    a, b = (neg, ts) if sign > 0 else (ts, neg)
    n = ch.shape[0]
    rows = jnp.concatenate([jnp.concatenate(tc + a, axis=1), jnp.concatenate(b + tc, axis=1)], axis=0)
    cols = jnp.concatenate([jnp.concatenate(tc + a, axis=0), jnp.concatenate(b + tc, axis=0)], axis=1)
    mid = []
    for re, im in pairs:
        r, i = split(re), split(im)
        v = mm(rows, jnp.concatenate([r[0], r[1], r[0], i[0], i[1], i[0]], axis=0))
        r, i = split(v[:n]), split(v[n:])
        mid.append(jnp.concatenate([r[0], r[1], r[0], i[0], i[1], i[0]], axis=1))
    v = mm(jnp.concatenate(mid, axis=0), cols)
    return [(v[j * n : (j + 1) * n, :n], v[j * n : (j + 1) * n, n:]) for j in range(len(pairs))]


MESH = pl.DeviceIdType.MESH
NX_, NYL, NYH, NZ, NK = 4, 4, 2, 12, 2
NY_ = NYL * NYH


def place():
    r, c = lax.axis_index("row"), lax.axis_index("col")
    y = lax.rem(lax.div(c, NK), NYH) * NYL + lax.div(r, NX_)
    return lax.rem(r, NX_), y, lax.div(c, NK * NYH), lax.rem(c, NK)


def device(x, y, z, k):
    row = lax.rem(y, NYL) * NX_ + x
    return {"row": row, "col": z * (NK * NYH) + lax.div(y, NYL) * NK + k}


def up(i, d, n):
    return lax.rem(i + d, n)


def send(src, dst, ss, rs, to):
    copy = copy_to(src, dst, ss, rs, to)
    copy.start()
    return copy


def shift_table(offset, wide, n):
    rows = lax.broadcasted_iota(jnp.int32, (wide, n), 0)
    cols = lax.broadcasted_iota(jnp.int32, (wide, n), 1)
    return jnp.where(rows == cols + offset, 1.0, 0.0).astype(BF16)


def select_table(offset, n, wide):
    rows = lax.broadcasted_iota(jnp.int32, (n, wide), 0)
    cols = lax.broadcasted_iota(jnp.int32, (n, wide), 1)
    return jnp.where(cols == rows + offset, 1.0, 0.0).astype(BF16)


def patch_of(high, low, y, x, n):
    rows = select_table(y, n, 2 * n)
    cols = shift_table(x, 2 * n, n)
    out = []
    for part in range(2):
        h = mm(rows, high[part]).astype(BF16)
        l = mm(rows, low[part]).astype(BF16)
        out.append(mm(h, cols) + mm(l, cols))
    return out


def place_terms(terms, ys, xs, n):
    scans = len(ys)
    rows = jnp.concatenate([shift_table(y, 2 * n, n) for y in ys] * 2, axis=1)
    cols = [select_table(x, n, 2 * n) for x in xs]
    out = []
    for part in range(2):
        high, low = [], []
        for scan in range(scans):
            h, l = split(terms[scan][part])
            high.append(mm(h, cols[scan]).astype(BF16))
            low.append(mm(l, cols[scan]).astype(BF16))
        out.append(mm(rows, jnp.concatenate(high + low, axis=0)))
    return out


class ProbeSum:
    def __init__(self, p, out, base, rows, where, bufs, sems, scale):
        self.p, self.out, self.base, self.scale = p, out, base, scale
        self.x, self.y, self.z, self.k = self.where = where
        self.half = rows // NK
        self.xb = self.half // NX_
        self.yb = self.xb // NY_
        self.cin, self.acc, self.xin, self.ysum, self.yin, self.zin = bufs
        self.sems = sems
        x, y, z, k = where
        self.sibling = device(x, y, z, 1 - k)
        self.xpeer = [device(up(x, d, NX_), y, z, k) for d in range(1, NX_)]
        self.ypeer = [device(x, up(y, d, NY_), z, k) for d in range(1, NY_)]
        self.zpeer = [device(x, y, up(z, d, NZ), k) for d in range(1, NZ)]
        self.order = [up(x, d, NX_) for d in range(1, NX_ + 1)]
        self.own = base + k * self.half + x * self.xb + y * self.yb

    def rows(self, start, size):
        return pl.ds(pl.multiple_of(start, 8), size)

    def start(self):
        s, r = self.sems[0]
        other = self.base + (1 - self.k) * self.half
        self.core = [
            send(self.p.at[self.rows(other + j * self.xb, self.xb)], self.cin.at[self.rows(j * self.xb, self.xb)], s.at[d], r.at[d], self.sibling)
            for d, j in enumerate(self.order)
        ]

    def along_x(self):
        s, r = self.sems[1]
        self.xc = []
        for d, j in enumerate(self.order):
            self.core[d].wait_recv()
            rows = self.rows(j * self.xb, self.xb)
            self.acc[rows] = self.p[self.rows(self.base + self.k * self.half + j * self.xb, self.xb)] + self.cin[rows]
            if d < NX_ - 1:
                self.xc.append(send(self.acc.at[rows], self.xin.at[d], s.at[d], r.at[d], self.xpeer[d]))

    def along_y(self):
        s, r = self.sems[2]
        for copy in self.xc:
            copy.wait_recv()
        self.yc = []
        for d in range(1, NY_ + 1):
            j = up(self.y, d, NY_)
            rows = self.rows(j * self.yb, self.yb)
            v = self.acc[self.rows(self.x * self.xb + j * self.yb, self.yb)]
            for i in range(NX_ - 1):
                v += self.xin[i, rows]
            self.ysum[rows] = v
            if d < NY_:
                self.yc.append(send(self.ysum.at[rows], self.yin.at[d - 1], s.at[d - 1], r.at[d - 1], self.ypeer[d - 1]))

    def along_z(self):
        s, r = self.sems[3]
        v = self.ysum[self.rows(self.y * self.yb, self.yb)]
        for i, copy in enumerate(self.yc):
            copy.wait_recv()
            v += self.yin[i]
        self.zin[self.z] = v
        self.zc = [send(self.zin.at[self.z], self.zin.at[self.z], s.at[d], r.at[d], self.zpeer[d]) for d in range(NZ - 1)]

    def pass_on(self, e, rows):
        s, r = self.sems[5]
        self.xg.append([send(self.out.at[rows], self.out.at[rows], s.at[e, d], r.at[e, d], self.xpeer[d]) for d in range(NX_ - 1)])

    def to_sibling(self, e, rows):
        s, r = self.sems[6]
        self.cg.append(send(self.out.at[rows], self.out.at[rows], s.at[e], r.at[e], self.sibling))

    def back_y(self):
        s, r = self.sems[4]
        for copy in self.zc:
            copy.wait_recv()
        v = self.zin[0]
        for i in range(1, NZ):
            v += self.zin[i]
        own = self.rows(self.own, self.yb)
        self.out[own] = v * self.scale
        self.yg = [send(self.out.at[own], self.out.at[own], s.at[d], r.at[d], self.ypeer[d]) for d in range(NY_ - 1)]
        self.xg, self.cg = [], []
        self.pass_on(0, own)

    def back_x(self):
        line = self.base + self.k * self.half
        for e in range(1, NY_):
            self.yg[e - 1].wait_recv()
            self.pass_on(e, self.rows(line + self.x * self.xb + up(self.y, NY_ - e, NY_) * self.yb, self.yb))
        self.to_sibling(0, self.rows(line + self.x * self.xb, self.xb))

    def back_core(self):
        line = self.base + self.k * self.half
        for d in range(NX_ - 1):
            for e in range(NY_):
                self.xg[e][d].wait_recv()
            self.to_sibling(d + 1, self.rows(line + up(self.x, NX_ - 1 - d, NX_) * self.xb, self.xb))

    def finish(self):
        for copy in self.cg:
            copy.wait_recv()
        for copy in self.core + self.xc + self.yc + self.zc + self.yg + [v for g in self.xg for v in g] + self.cg:
            copy.wait_send()


def gradients_kernel(scale, down, across, region, probe, measured, tables, tile, out, spread, patches, wave, terms, p,
                     left_in, above_in, side_in, corner_in, under_sum, right_sum, via, cin, acc, xin, ysum, yin, zin,
                     ls, lr, as_, ar, ss, sr, ks, kr, vr, fs, *sums):
    n = probe.shape[-1]
    modes, scans = probe.shape[0], measured.shape[0]
    r, c = lax.axis_index("row"), lax.axis_index("col")
    last_row = NX_ * NYL - 1
    x, y, z, k = place()
    per_mode = 2 * n
    probe_sums = [
        ProbeSum(p, out, m * per_mode, per_mode, (x, y, z, k), [v.at[m] for v in (cin, acc, xin, ysum, yin, zin)],
                 [(sums[2 * i].at[m], sums[2 * i + 1].at[m]) for i in range(len(sums) // 2)], scale)
        for m in range(modes)
    ]
    first, second = probe_sums
    sibling, xpeer, ypeer, zpeer = first.sibling, first.xpeer, first.ypeer, first.zpeer
    above, below, leftward, rightward = neighbours()
    y_lo = lax.div(r, NX_)
    detours = (x == NX_ - 1) & (r < last_row)
    passes = (x == 0) & (y_lo < NYL - 1)
    detour = {"row": lax.rem(r + NX_ * NYL - (NX_ - 1), NX_ * NYL), "col": c}
    onward = {"row": lax.rem(r + NX_, NX_ * NYL), "col": c}
    sources = [{"row": lax.rem(r + d, NX_ * NYL), "col": c} for d in (NX_ - 1, NX_ * NYL - NX_)]
    peers = [sibling, above, below, leftward, rightward] + sources + xpeer + ypeer + zpeer
    greet(peers)


    lo, hi = pl.ds(0, n), pl.ds(n, n)
    side_right = copy_to(spread.at[:, lo, hi], left_in, ls.at[0], lr.at[0], sibling)
    side_under = copy_to(spread.at[:, hi, hi], side_in, ss, sr, sibling)
    cut = pieces(n)
    middle = len(cut) // 2
    under, under_round, under_pass, corners, corner_round, corner_pass, rights, firsts = [[] for _ in range(8)]
    for i, (q, h, s) in enumerate(cut):
        rows = pl.ds(h, s)
        below_left, below_right = under_sum.at[q, rows], spread.at[q, pl.ds(n + h, s), hi]
        under.append(copy_to(below_left, above_in.at[q, rows], as_.at[i], ar.at[i], below))
        corners.append(copy_to(below_right, corner_in.at[q, rows], ks.at[i], kr.at[i], below))
        rights.append(copy_to(right_sum.at[q, rows], left_in.at[q, rows], ls.at[i], lr.at[i], rightward))
        firsts.append(copy_to(spread.at[q, rows, hi], left_in.at[q, rows], ls.at[i], lr.at[i], rightward))
        if i >= middle:
            e, f = i - middle, i
            under_round.append(copy_to(below_left, via.at[e], as_.at[i], vr.at[e], detour))
            corner_round.append(copy_to(below_right, via.at[f], ks.at[i], vr.at[f], detour))
            under_pass.append(copy_to(via.at[e], above_in.at[q, rows], fs.at[e], ar.at[i], onward))
            corner_pass.append(copy_to(via.at[f], corner_in.at[q, rows], fs.at[f], kr.at[i], onward))

    def downward(direct, rounds):
        for i in list(range(middle, len(cut))) + list(range(middle)):
            if i < middle:
                pl.when(r < last_row)(direct[i].start)
            else:
                pl.when((r < last_row) & (x < NX_ - 1))(direct[i].start)
                pl.when(detours)(rounds[i - middle].start)

    def pass_down(rounds, passing):
        @pl.when(passes)
        def _():
            for e in range(middle):
                rounds[e].wait_recv()
                passing[e].start()

    c_table, s_table = (tables[0], tables[1]), (tables[2], tables[3])
    ys = [down[scan] for scan in range(scans)]
    xs = [across[scan] for scan in range(scans)]
    high, low = zip(*[split(region[part]) for part in range(2)])
    for scan in range(scans):
        pr, pi = patch_of(high, low, ys[scan], xs[scan], n)
        patches[scan, 0], patches[scan, 1] = pr, pi
        exits = []
        for m in range(modes):
            mr, mi = probe[m, 0], probe[m, 1]
            exits.append((mr * pr - mi * pi, mr * pi + mi * pr))
        waves = transform(c_table, s_table, exits, -1.0)
        resid = -measured[scan]
        for wr, wi in waves:
            resid += wr * wr + wi * wi
        for m, (wr, wi) in enumerate(waves):
            wave[m, scan, 0], wave[m, scan, 1] = resid * wr, resid * wi
    for m in range(modes):
        backs = transform(c_table, s_table, [(wave[m, scan, 0], wave[m, scan, 1]) for scan in range(scans)], 1.0)
        mr, mi = probe[m, 0], probe[m, 1]
        qr = qi = 0.0
        for scan, (br, bi) in enumerate(backs):
            tr, ti = mr * br + mi * bi, mr * bi - mi * br
            if m == 0:
                terms[scan, 0], terms[scan, 1] = tr, ti
            else:
                terms[scan, 0] += tr
                terms[scan, 1] += ti
            pr, pi = patches[scan, 0], patches[scan, 1]
            qr += pr * br + pi * bi
            qi += pr * bi - pi * br
        p[m * per_mode : m * per_mode + n, :] = qr
        p[m * per_mode + n : (m + 1) * per_mode, :] = qi
        if m == 0:
            meet(peers)
        probe_sums[m].start()
        if m == 1:
            first.along_x()
    placed = place_terms([(terms[scan, 0], terms[scan, 1]) for scan in range(scans)], ys, xs, n)
    for part in range(2):
        spread[part] = placed[part]

    @pl.when(k == 0)
    def _():
        side_under.start()
        side_right.start()

    @pl.when(k == 1)
    def _():
        downward(corners, corner_round)

    @pl.when((k == 1) & (r == 0))
    def _():
        for copy in firsts:
            copy.start()

    second.along_x()
    first.along_y()

    @pl.when(k == 0)
    def _():
        under_sum[...] = spread[:, n:, :n]

    @pl.when(k == 1)
    def _():
        side_under.wait_recv()
        under_sum[...] = spread[:, n:, :n] + side_in[...]

    first.along_z()
    second.along_y()
    downward(under, under_round)

    @pl.when(k == 1)
    def _():
        pass_down(corner_round, corner_pass)

    @pl.when((k == 1) & (r > 0))
    def _():
        for i, (q, h, s) in enumerate(cut):
            corners[i].wait_recv()
            right_sum[q, h : h + s] = spread[q, h : h + s, n:] + corner_in[q, h : h + s]
            rights[i].start()

    second.along_z()
    pass_down(under_round, under_pass)
    first.back_y()
    second.back_y()
    first.back_x()
    second.back_x()

    @pl.when(r > 0)
    def _():
        for copy in under:
            copy.wait_recv()
        tile[...] = spread[:, :n, :n] + above_in[...]

    @pl.when(r == 0)
    def _():
        tile[...] = spread[:, :n, :n]

    @pl.when(k == 1)
    def _():
        side_right.wait_recv()

    @pl.when(k == 0)
    def _():
        for copy in rights:
            copy.wait_recv()

    @pl.when(c > 0)
    def _():
        tile[...] += left_in[...]

    first.back_core()
    second.back_core()
    first.finish()
    second.finish()

    @pl.when(k == 0)
    def _():
        side_under.wait_send()
        side_right.wait_send()

    @pl.when(k == 1)
    def _():
        for copy in rights:
            copy.wait_send()

    @pl.when(passes)
    def _():
        for copy in under_pass:
            copy.wait_send()

        @pl.when(k == 1)
        def _():
            for copy in corner_pass:
                copy.wait_send()

    @pl.when(r < last_row)
    def _():
        for copy in under:
            copy.wait_send()

        @pl.when(k == 1)
        def _():
            for copy in corners:
                copy.wait_send()


def gradients(down, across, region, probe, measured, scale):
    modes, _, n, _ = probe.shape
    scans = measured.shape[0]
    half = 2 * n // NK
    xb = half // NX_
    yb = xb // NY_
    dma = pltpu.SemaphoreType.DMA
    pairs = [(4,), (4,), (), (4,), (4,)]
    pairs += [(modes, *s) for s in ((NX_,), (NX_ - 1,), (NY_ - 1,), (NZ - 1,), (NY_ - 1,), (NY_, NX_ - 1), (NX_,))]
    vm = pl.BlockSpec(memory_space=pltpu.VMEM)
    sm = pl.BlockSpec(memory_space=pltpu.SMEM)

    def f32(*shape):
        return pltpu.VMEM(shape, F32)

    tile, out = pl.pallas_call(
        functools.partial(gradients_kernel, scale),
        out_shape=[jax.ShapeDtypeStruct((2, n, n), F32), jax.ShapeDtypeStruct((modes * 2 * n, n), F32)],
        in_specs=[sm, sm, vm, vm, vm, vm],
        out_specs=[vm, vm],
        scratch_shapes=[
            f32(2, 2 * n, 2 * n),
            f32(scans, 2, n, n),
            f32(modes, scans, 2, n, n),
            f32(scans, 2, n, n),
            f32(modes * 2 * n, n),
        ]
        + [f32(2, n, n)] * 6
        + [
            f32(4, n // 2, n),
            f32(modes, half, n),
            f32(modes, half, n),
            f32(modes, NX_ - 1, xb, n),
            f32(modes, xb, n),
            f32(modes, NY_ - 1, yb, n),
            f32(modes, NZ, yb, n),
        ]
        + [dma(s) for s in pairs for _ in range(2)],
        compiler_params=pltpu.CompilerParams(
            collective_id=0, has_side_effects=True, vmem_limit_bytes=28 * 1024 * 1024
        ),
    )(down, across, region, probe, measured, dft_tables(n))
    return tile, out.reshape(probe.shape)


def neighbours():
    r, c = lax.axis_index("row"), lax.axis_index("col")
    rows, cols = NX_ * NYL, NZ * NYH * NK
    above = {"row": lax.rem(r + rows - 1, rows), "col": c}
    below = {"row": lax.rem(r + 1, rows), "col": c}
    leftward = {"row": r, "col": lax.rem(c + cols - 1, cols)}
    rightward = {"row": r, "col": lax.rem(c + 1, cols)}
    return above, below, leftward, rightward


def greet(peers):
    barrier = pltpu.get_barrier_semaphore()
    for peer in peers:
        pl.semaphore_signal(barrier, inc=1, device_id=peer, device_id_type=MESH)


def meet(peers):
    pl.semaphore_wait(pltpu.get_barrier_semaphore(), len(peers))


def copy_to(src, dst, ss, rs, to):
    return pltpu.make_async_remote_copy(
        src_ref=src, dst_ref=dst, send_sem=ss, recv_sem=rs, device_id=to, device_id_type=MESH
    )


def pieces(n):
    return [(part, h * (n // 2), n // 2) for part in range(2) for h in range(2)]


def gather_kernel(t, region, via, rs_, rr, bs, br, ds, dr, vr, fs):
    n = t.shape[-1]
    r, c = lax.axis_index("row"), lax.axis_index("col")
    last_row, last_col = NX_ * NYL - 1, NZ * NYH * NK - 1
    k, x, y_lo = lax.rem(c, NK), lax.rem(r, NX_), lax.div(r, NX_)
    above, below, leftward, rightward = neighbours()
    detours = (x == 0) & (r > 0)
    passes = (x == NX_ - 1) & (y_lo > 0)
    detour = {"row": lax.rem(r + NX_ - 1, NX_ * NYL), "col": c}
    onward = {"row": lax.rem(r + NX_ * NYL - NX_, NX_ * NYL), "col": c}
    sources = [{"row": lax.rem(r + d, NX_ * NYL), "col": c} for d in (NX_ * NYL - NX_ + 1, NX_)]
    peers = [above, below, leftward, rightward] + sources
    greet(peers)
    meet(peers)

    left_part = pl.ds(0, n)
    right_part = pl.ds(n, n)
    cut = pieces(n)
    half = len(cut) // 2
    to_left, to_above, on_above, on_sibling = [], [], [], []
    round_above, round_on, pass_above, pass_on = [], [], [], []
    for i, (p, h, s) in enumerate(cut):
        own = t.at[p, pl.ds(h, s)]
        right = region.at[p, pl.ds(h, s), right_part]
        under = region.at[p, pl.ds(n + h, s), left_part]
        corner = region.at[p, pl.ds(n + h, s), right_part]
        to_left.append(copy_to(own, right, rs_.at[i], rr.at[i], leftward))
        to_above.append(copy_to(own, under, bs.at[i], br.at[i], above))
        on_above.append(copy_to(right, corner, ds.at[i], dr.at[i], above))
        on_sibling.append(copy_to(under, corner, ds.at[i], dr.at[i], leftward))
        if i >= half:
            a, b = i - half, i
            round_above.append(copy_to(own, via.at[a], bs.at[i], vr.at[a], detour))
            round_on.append(copy_to(right, via.at[b], ds.at[i], vr.at[b], detour))
            pass_above.append(copy_to(via.at[a], under, fs.at[a], br.at[i], onward))
            pass_on.append(copy_to(via.at[b], corner, fs.at[b], dr.at[i], onward))

    def upward(direct, rounds, i):
        if i < half:
            pl.when(r > 0)(direct[i].start)
        else:
            pl.when((r > 0) & (x > 0))(direct[i].start)
            pl.when(detours)(rounds[i - half].start)

    for i in range(len(cut)):
        to_left[i].start()
    for i in range(len(cut)):
        upward(to_above, round_above, i)
    region[:, :n, :n] = t[...]

    @pl.when(r == last_row)
    def _():
        region[:, n:, :] = jnp.zeros((2, n, 2 * n), F32)

    def pass_first():
        for a in range(half):
            round_above[a].wait_recv()
            pass_above[a].start()

    @pl.when(k == 1)
    def _():
        for i in range(len(cut)):
            @pl.when(r < last_row)
            def _():
                to_above[i].wait_recv()
                on_sibling[i].start()

            to_left[i].wait_recv()
            upward(on_above, round_on, i)
            if i == half - 1:
                pl.when(passes)(pass_first)

        @pl.when(passes)
        def _():
            for a in range(half):
                round_on[a].wait_recv()
                pass_on[a].start()

        for i in range(len(cut)):
            @pl.when(r < last_row)
            def _():
                on_above[i].wait_recv()
                on_sibling[i].wait_send()

            @pl.when(r > 0)
            def _():
                on_above[i].wait_send()

        @pl.when(passes)
        def _():
            for a in range(half):
                pass_on[a].wait_send()

    @pl.when(k == 0)
    def _():
        pl.when(passes)(pass_first)
        for i in range(len(cut)):
            to_left[i].wait_recv()

            @pl.when(r < last_row)
            def _():
                to_above[i].wait_recv()
                on_sibling[i].wait_recv()

    for i in range(len(cut)):
        to_left[i].wait_send()
        pl.when(r > 0)(to_above[i].wait_send)

    @pl.when(passes)
    def _():
        for a in range(half):
            pass_above[a].wait_send()

    @pl.when(c == last_col)
    def _():
        region[:, :, n:] = jnp.zeros((2, 2 * n, n), F32)


def gather_region(tile):
    n = tile.shape[-1]
    vm = pl.BlockSpec(memory_space=pltpu.VMEM)
    return pl.pallas_call(
        gather_kernel,
        out_shape=jax.ShapeDtypeStruct((2, 2 * n, 2 * n), F32),
        in_specs=[vm],
        out_specs=vm,
        scratch_shapes=[pltpu.VMEM((4, n // 2, n), F32)] + [pltpu.SemaphoreType.DMA((4,))] * 8,
        compiler_params=pltpu.CompilerParams(
            collective_id=1, has_side_effects=True, vmem_limit_bytes=12 * 1024 * 1024
        ),
    )(tile)


def on_device(transmission, probe_modes, measured, offset_down, offset_across):
    region = gather_region(transmission)
    scans = measured.shape[0] * lax.axis_size("row") * lax.axis_size("col")
    return gradients(offset_down, offset_across, region, probe_modes, measured, 1.0 / math.sqrt(scans))


def solution(mesh):
    in_specs = (
        P(None, "row", "col"),
        P(),
        P(("row", "col"), None, None),
        P(("row", "col")),
        P(("row", "col")),
    )
    out_specs = (P(None, "row", "col"), P())
    return jax.shard_map(
        on_device, mesh=mesh, in_specs=in_specs, out_specs=out_specs, check_vma=False
    )
```

```python
import functools
import math
import numpy as np
import jax
import jax.numpy as jnp
from jax import lax
from jax.experimental import pallas as pl
from jax.experimental.pallas import tpu as pltpu
from jax.sharding import PartitionSpec as P

F32, BF16 = jnp.float32, jnp.bfloat16


def split(v):
    high = v.astype(BF16)
    return high, (v - high.astype(F32)).astype(BF16)


def dft_tables(n):
    counter = np.arange(n)
    angles = (counter[:, None] * counter[None, :] % n) * (2.0 * math.pi / n)
    out = []
    for t in (np.cos(angles), np.sin(angles)):
        t = jnp.asarray((t / math.sqrt(n)).astype(np.float32))
        out += list(split(t))
    return jnp.stack(out)


def mm(a, b):
    return jnp.dot(a, b, preferred_element_type=F32)


def transform(c, s, pairs, sign):
    ch, cl = c
    sh, sl = s
    tc = [ch, ch, cl]
    ts = [sh, sh, sl]
    neg = [-sh, -sh, -sl]
    a, b = (neg, ts) if sign > 0 else (ts, neg)
    n = ch.shape[0]
    rows = jnp.concatenate([jnp.concatenate(tc + a, axis=1), jnp.concatenate(b + tc, axis=1)], axis=0)
    cols = jnp.concatenate([jnp.concatenate(tc + a, axis=0), jnp.concatenate(b + tc, axis=0)], axis=1)
    mid = []
    for re, im in pairs:
        r, i = split(re), split(im)
        v = mm(rows, jnp.concatenate([r[0], r[1], r[0], i[0], i[1], i[0]], axis=0))
        r, i = split(v[:n]), split(v[n:])
        mid.append(jnp.concatenate([r[0], r[1], r[0], i[0], i[1], i[0]], axis=1))
    v = mm(jnp.concatenate(mid, axis=0), cols)
    return [(v[j * n : (j + 1) * n, :n], v[j * n : (j + 1) * n, n:]) for j in range(len(pairs))]


MESH = pl.DeviceIdType.MESH
NX_, NYL, NYH, NZ, NK = 4, 4, 2, 12, 2
NY_ = NYL * NYH
CUTS = 4


def place():
    r, c = lax.axis_index("row"), lax.axis_index("col")
    y = lax.rem(lax.div(c, NK), NYH) * NYL + lax.div(r, NX_)
    return lax.rem(r, NX_), y, lax.div(c, NK * NYH), lax.rem(c, NK)


def device(x, y, z, k):
    row = lax.rem(y, NYL) * NX_ + x
    return {"row": row, "col": z * (NK * NYH) + lax.div(y, NYL) * NK + k}


def up(i, d, n):
    return lax.rem(i + d, n)


def send(src, dst, ss, rs, to):
    copy = copy_to(src, dst, ss, rs, to)
    copy.start()
    return copy


def shift_table(offset, wide, n):
    rows = lax.broadcasted_iota(jnp.int32, (wide, n), 0)
    cols = lax.broadcasted_iota(jnp.int32, (wide, n), 1)
    return jnp.where(rows == cols + offset, 1.0, 0.0).astype(BF16)


def select_table(offset, n, wide):
    rows = lax.broadcasted_iota(jnp.int32, (n, wide), 0)
    cols = lax.broadcasted_iota(jnp.int32, (n, wide), 1)
    return jnp.where(cols == rows + offset, 1.0, 0.0).astype(BF16)


def patch_of(high, low, y, x, n):
    rows = select_table(y, n, 2 * n)
    cols = shift_table(x, 2 * n, n)
    out = []
    for part in range(2):
        h = mm(rows, high[part]).astype(BF16)
        l = mm(rows, low[part]).astype(BF16)
        out.append(mm(h, cols) + mm(l, cols))
    return out


def place_terms(terms, ys, xs, n):
    scans = len(ys)
    rows = jnp.concatenate([shift_table(y, 2 * n, n) for y in ys] * 2, axis=1)
    cols = [select_table(x, n, 2 * n) for x in xs]
    out = []
    for part in range(2):
        high, low = [], []
        for scan in range(scans):
            h, l = split(terms[scan][part])
            high.append(mm(h, cols[scan]).astype(BF16))
            low.append(mm(l, cols[scan]).astype(BF16))
        out.append(mm(rows, jnp.concatenate(high + low, axis=0)))
    return out


class ProbeSum:
    def __init__(self, p, out, base, rows, where, bufs, sems, scale):
        self.p, self.out, self.base, self.scale = p, out, base, scale
        self.x, self.y, self.z, self.k = self.where = where
        self.half = rows // NK
        self.xb = self.half // NX_
        self.yb = self.xb // NY_
        self.cin, self.acc, self.xin, self.ysum, self.yin, self.zin = bufs
        self.sems = sems
        x, y, z, k = where
        self.sibling = device(x, y, z, 1 - k)
        self.xpeer = [device(up(x, d, NX_), y, z, k) for d in range(1, NX_)]
        self.ypeer = [device(x, up(y, d, NY_), z, k) for d in range(1, NY_)]
        self.zpeer = [device(x, y, up(z, d, NZ), k) for d in range(1, NZ)]
        self.order = [up(x, d, NX_) for d in range(1, NX_ + 1)]
        self.own = base + k * self.half + x * self.xb + y * self.yb

    def rows(self, start, size):
        return pl.ds(pl.multiple_of(start, 8), size)

    def start(self):
        s, r = self.sems[0]
        other = self.base + (1 - self.k) * self.half
        self.core = [
            send(self.p.at[self.rows(other + j * self.xb, self.xb)], self.cin.at[self.rows(j * self.xb, self.xb)], s.at[d], r.at[d], self.sibling)
            for d, j in enumerate(self.order)
        ]

    def along_x(self):
        s, r = self.sems[1]
        self.xc = []
        for d, j in enumerate(self.order):
            self.core[d].wait_recv()
            rows = self.rows(j * self.xb, self.xb)
            self.acc[rows] = self.p[self.rows(self.base + self.k * self.half + j * self.xb, self.xb)] + self.cin[rows]
            if d < NX_ - 1:
                self.xc.append(send(self.acc.at[rows], self.xin.at[d], s.at[d], r.at[d], self.xpeer[d]))

    def along_y(self):
        s, r = self.sems[2]
        for copy in self.xc:
            copy.wait_recv()
        self.yc = []
        for d in range(1, NY_ + 1):
            j = up(self.y, d, NY_)
            rows = self.rows(j * self.yb, self.yb)
            v = self.acc[self.rows(self.x * self.xb + j * self.yb, self.yb)]
            for i in range(NX_ - 1):
                v += self.xin[i, rows]
            self.ysum[rows] = v
            if d < NY_:
                self.yc.append(send(self.ysum.at[rows], self.yin.at[d - 1], s.at[d - 1], r.at[d - 1], self.ypeer[d - 1]))

    def along_z(self):
        s, r = self.sems[3]
        v = self.ysum[self.rows(self.y * self.yb, self.yb)]
        for i, copy in enumerate(self.yc):
            copy.wait_recv()
            v += self.yin[i]
        self.zin[self.z] = v
        self.zc = [send(self.zin.at[self.z], self.zin.at[self.z], s.at[d], r.at[d], self.zpeer[d]) for d in range(NZ - 1)]

    def to_sibling(self, e, rows):
        s, r = self.sems[6]
        self.cg.append(send(self.out.at[rows], self.out.at[rows], s.at[e], r.at[e], self.sibling))

    def back_y(self):
        s, r = self.sems[4]
        for copy in self.zc:
            copy.wait_recv()
        v = self.zin[0]
        for i in range(1, NZ):
            v += self.zin[i]
        own = self.rows(self.own, self.yb)
        self.out[own] = v * self.scale
        self.yg = [send(self.out.at[own], self.out.at[own], s.at[d], r.at[d], self.ypeer[d]) for d in range(NY_ - 1)]
        self.cg = []

    def back_x(self):
        s, r = self.sems[5]
        for copy in self.yg:
            copy.wait_recv()
        rows = self.rows(self.base + self.k * self.half + self.x * self.xb, self.xb)
        self.xg = [send(self.out.at[rows], self.out.at[rows], s.at[d], r.at[d], self.xpeer[d]) for d in range(NX_ - 1)]
        self.to_sibling(0, rows)

    def back_core(self):
        line = self.base + self.k * self.half
        for d in range(NX_ - 1):
            self.xg[d].wait_recv()
            self.to_sibling(d + 1, self.rows(line + up(self.x, NX_ - 1 - d, NX_) * self.xb, self.xb))

    def finish(self):
        for copy in self.cg:
            copy.wait_recv()
        for copy in self.core + self.xc + self.yc + self.zc + self.yg + self.xg + self.cg:
            copy.wait_send()


def gradients_kernel(scale, down, across, region, probe, measured, tables, tile, out, spread, patches, wave, terms, p,
                     left_in, above_in, side_in, corner_in, under_sum, right_sum, via, cin, acc, xin, ysum, yin, zin,
                     ls, lr, as_, ar, ss, sr, ks, kr, vr, fs, *sums):
    n = probe.shape[-1]
    modes, scans = probe.shape[0], measured.shape[0]
    r, c = lax.axis_index("row"), lax.axis_index("col")
    last_row = NX_ * NYL - 1
    x, y, z, k = place()
    per_mode = 2 * n
    probe_sums = [
        ProbeSum(p, out, m * per_mode, per_mode, (x, y, z, k), [v.at[m] for v in (cin, acc, xin, ysum, yin, zin)],
                 [(sums[2 * i].at[m], sums[2 * i + 1].at[m]) for i in range(len(sums) // 2)], scale)
        for m in range(modes)
    ]
    first, second = probe_sums
    sibling, xpeer, ypeer, zpeer = first.sibling, first.xpeer, first.ypeer, first.zpeer
    above, below, leftward, rightward = neighbours()
    y_lo = lax.div(r, NX_)
    detours = (x == NX_ - 1) & (r < last_row)
    passes = (x == 0) & (y_lo < NYL - 1)
    detour = {"row": lax.rem(r + NX_ * NYL - (NX_ - 1), NX_ * NYL), "col": c}
    onward = {"row": lax.rem(r + NX_, NX_ * NYL), "col": c}
    sources = [{"row": lax.rem(r + d, NX_ * NYL), "col": c} for d in (NX_ - 1, NX_ * NYL - NX_)]
    peers = [sibling, above, below, leftward, rightward] + sources + xpeer + ypeer + zpeer
    greet(peers)


    lo, hi = pl.ds(0, n), pl.ds(n, n)
    side_right = copy_to(spread.at[:, lo, hi], left_in, ls.at[0], lr.at[0], sibling)
    side_under = copy_to(spread.at[:, hi, hi], side_in, ss, sr, sibling)
    cut = pieces(n)
    middle = len(cut) // 2
    under, under_round, under_pass, corners, corner_round, corner_pass, rights, firsts = [[] for _ in range(8)]
    for i, (q, h, s) in enumerate(cut):
        rows = pl.ds(h, s)
        below_left, below_right = under_sum.at[q, rows], spread.at[q, pl.ds(n + h, s), hi]
        under.append(copy_to(below_left, above_in.at[q, rows], as_.at[i], ar.at[i], below))
        corners.append(copy_to(below_right, corner_in.at[q, rows], ks.at[i], kr.at[i], below))
        rights.append(copy_to(right_sum.at[q, rows], left_in.at[q, rows], ls.at[i], lr.at[i], rightward))
        firsts.append(copy_to(spread.at[q, rows, hi], left_in.at[q, rows], ls.at[i], lr.at[i], rightward))
        if i >= middle:
            e, f = i - middle, i
            under_round.append(copy_to(below_left, via.at[e], as_.at[i], vr.at[e], detour))
            corner_round.append(copy_to(below_right, via.at[f], ks.at[i], vr.at[f], detour))
            under_pass.append(copy_to(via.at[e], above_in.at[q, rows], fs.at[e], ar.at[i], onward))
            corner_pass.append(copy_to(via.at[f], corner_in.at[q, rows], fs.at[f], kr.at[i], onward))

    def downward(direct, rounds):
        for i in list(range(middle, len(cut))) + list(range(middle)):
            if i < middle:
                pl.when(r < last_row)(direct[i].start)
            else:
                pl.when((r < last_row) & (x < NX_ - 1))(direct[i].start)
                pl.when(detours)(rounds[i - middle].start)

    def pass_down(rounds, passing):
        @pl.when(passes)
        def _():
            for e in range(middle):
                rounds[e].wait_recv()
                passing[e].start()

    c_table, s_table = (tables[0], tables[1]), (tables[2], tables[3])
    ys = [down[scan] for scan in range(scans)]
    xs = [across[scan] for scan in range(scans)]
    high, low = zip(*[split(region[part]) for part in range(2)])
    for scan in range(scans):
        pr, pi = patch_of(high, low, ys[scan], xs[scan], n)
        patches[scan, 0], patches[scan, 1] = pr, pi
        exits = []
        for m in range(modes):
            mr, mi = probe[m, 0], probe[m, 1]
            exits.append((mr * pr - mi * pi, mr * pi + mi * pr))
        waves = transform(c_table, s_table, exits, -1.0)
        resid = -measured[scan]
        for wr, wi in waves:
            resid += wr * wr + wi * wi
        for m, (wr, wi) in enumerate(waves):
            wave[m, scan, 0], wave[m, scan, 1] = resid * wr, resid * wi
    for m in range(modes):
        backs = transform(c_table, s_table, [(wave[m, scan, 0], wave[m, scan, 1]) for scan in range(scans)], 1.0)
        mr, mi = probe[m, 0], probe[m, 1]
        qr = qi = 0.0
        for scan, (br, bi) in enumerate(backs):
            tr, ti = mr * br + mi * bi, mr * bi - mi * br
            if m == 0:
                terms[scan, 0], terms[scan, 1] = tr, ti
            else:
                terms[scan, 0] += tr
                terms[scan, 1] += ti
            pr, pi = patches[scan, 0], patches[scan, 1]
            qr += pr * br + pi * bi
            qi += pr * bi - pi * br
        p[m * per_mode : m * per_mode + n, :] = qr
        p[m * per_mode + n : (m + 1) * per_mode, :] = qi
        if m == 0:
            meet(peers)
        probe_sums[m].start()
        if m == 1:
            first.along_x()
    placed = place_terms([(terms[scan, 0], terms[scan, 1]) for scan in range(scans)], ys, xs, n)
    for part in range(2):
        spread[part] = placed[part]

    @pl.when(k == 0)
    def _():
        side_under.start()
        side_right.start()

    @pl.when(k == 1)
    def _():
        downward(corners, corner_round)

    @pl.when((k == 1) & (r == 0))
    def _():
        for copy in firsts:
            copy.start()

    second.along_x()
    first.along_y()

    @pl.when(k == 0)
    def _():
        under_sum[...] = spread[:, n:, :n]

    @pl.when(k == 1)
    def _():
        side_under.wait_recv()
        under_sum[...] = spread[:, n:, :n] + side_in[...]

    first.along_z()
    second.along_y()
    downward(under, under_round)

    @pl.when(k == 1)
    def _():
        pass_down(corner_round, corner_pass)

    @pl.when((k == 1) & (r > 0))
    def _():
        for i, (q, h, s) in enumerate(cut):
            corners[i].wait_recv()
            right_sum[q, h : h + s] = spread[q, h : h + s, n:] + corner_in[q, h : h + s]
            rights[i].start()

    second.along_z()
    pass_down(under_round, under_pass)
    first.back_y()
    second.back_y()
    first.back_x()
    second.back_x()

    first.back_core()
    second.back_core()

    @pl.when(r > 0)
    def _():
        for copy in under:
            copy.wait_recv()
        tile[...] = spread[:, :n, :n] + above_in[...]

    @pl.when(r == 0)
    def _():
        tile[...] = spread[:, :n, :n]

    @pl.when(k == 1)
    def _():
        side_right.wait_recv()

    @pl.when(k == 0)
    def _():
        for copy in rights:
            copy.wait_recv()

    @pl.when(c > 0)
    def _():
        tile[...] += left_in[...]

    first.finish()
    second.finish()

    @pl.when(k == 0)
    def _():
        side_under.wait_send()
        side_right.wait_send()

    @pl.when(k == 1)
    def _():
        for copy in rights:
            copy.wait_send()

    @pl.when(passes)
    def _():
        for copy in under_pass:
            copy.wait_send()

        @pl.when(k == 1)
        def _():
            for copy in corner_pass:
                copy.wait_send()

    @pl.when(r < last_row)
    def _():
        for copy in under:
            copy.wait_send()

        @pl.when(k == 1)
        def _():
            for copy in corners:
                copy.wait_send()


def gradients(down, across, region, probe, measured, scale):
    modes, _, n, _ = probe.shape
    scans = measured.shape[0]
    half = 2 * n // NK
    xb = half // NX_
    yb = xb // NY_
    dma = pltpu.SemaphoreType.DMA
    pairs = [(2 * CUTS,), (2 * CUTS,), (), (2 * CUTS,), (2 * CUTS,)]
    pairs += [(modes, *s) for s in ((NX_,), (NX_ - 1,), (NY_ - 1,), (NZ - 1,), (NY_ - 1,), (NX_ - 1,), (NX_,))]
    vm = pl.BlockSpec(memory_space=pltpu.VMEM)
    sm = pl.BlockSpec(memory_space=pltpu.SMEM)

    def f32(*shape):
        return pltpu.VMEM(shape, F32)

    tile, out = pl.pallas_call(
        functools.partial(gradients_kernel, scale),
        out_shape=[jax.ShapeDtypeStruct((2, n, n), F32), jax.ShapeDtypeStruct((modes * 2 * n, n), F32)],
        in_specs=[sm, sm, vm, vm, vm, vm],
        out_specs=[vm, vm],
        scratch_shapes=[
            f32(2, 2 * n, 2 * n),
            f32(scans, 2, n, n),
            f32(modes, scans, 2, n, n),
            f32(scans, 2, n, n),
            f32(modes * 2 * n, n),
        ]
        + [f32(2, n, n)] * 6
        + [
            f32(2 * CUTS, n // CUTS, n),
            f32(modes, half, n),
            f32(modes, half, n),
            f32(modes, NX_ - 1, xb, n),
            f32(modes, xb, n),
            f32(modes, NY_ - 1, yb, n),
            f32(modes, NZ, yb, n),
        ]
        + [dma(s) for s in pairs for _ in range(2)],
        compiler_params=pltpu.CompilerParams(
            collective_id=0, has_side_effects=True, vmem_limit_bytes=28 * 1024 * 1024
        ),
    )(down, across, region, probe, measured, dft_tables(n))
    return tile, out.reshape(probe.shape)


def neighbours():
    r, c = lax.axis_index("row"), lax.axis_index("col")
    rows, cols = NX_ * NYL, NZ * NYH * NK
    above = {"row": lax.rem(r + rows - 1, rows), "col": c}
    below = {"row": lax.rem(r + 1, rows), "col": c}
    leftward = {"row": r, "col": lax.rem(c + cols - 1, cols)}
    rightward = {"row": r, "col": lax.rem(c + 1, cols)}
    return above, below, leftward, rightward


def greet(peers):
    barrier = pltpu.get_barrier_semaphore()
    for peer in peers:
        pl.semaphore_signal(barrier, inc=1, device_id=peer, device_id_type=MESH)


def meet(peers):
    pl.semaphore_wait(pltpu.get_barrier_semaphore(), len(peers))


def copy_to(src, dst, ss, rs, to):
    return pltpu.make_async_remote_copy(
        src_ref=src, dst_ref=dst, send_sem=ss, recv_sem=rs, device_id=to, device_id_type=MESH
    )


def pieces(n):
    return [(part, h * (n // CUTS), n // CUTS) for part in range(2) for h in range(CUTS)]


def gather_kernel(t, region, via, rs_, rr, bs, br, ds, dr, vr, fs):
    n = t.shape[-1]
    r, c = lax.axis_index("row"), lax.axis_index("col")
    last_row, last_col = NX_ * NYL - 1, NZ * NYH * NK - 1
    k, x, y_lo = lax.rem(c, NK), lax.rem(r, NX_), lax.div(r, NX_)
    above, below, leftward, rightward = neighbours()
    detours = (x == 0) & (r > 0)
    passes = (x == NX_ - 1) & (y_lo > 0)
    detour = {"row": lax.rem(r + NX_ - 1, NX_ * NYL), "col": c}
    onward = {"row": lax.rem(r + NX_ * NYL - NX_, NX_ * NYL), "col": c}
    sources = [{"row": lax.rem(r + d, NX_ * NYL), "col": c} for d in (NX_ * NYL - NX_ + 1, NX_)]
    peers = [above, below, leftward, rightward] + sources
    greet(peers)
    meet(peers)

    left_part = pl.ds(0, n)
    right_part = pl.ds(n, n)
    cut = pieces(n)
    half = len(cut) // 2
    to_left, to_above, on_above, on_sibling = [], [], [], []
    round_above, round_on, pass_above, pass_on = [], [], [], []
    for i, (p, h, s) in enumerate(cut):
        own = t.at[p, pl.ds(h, s)]
        right = region.at[p, pl.ds(h, s), right_part]
        under = region.at[p, pl.ds(n + h, s), left_part]
        corner = region.at[p, pl.ds(n + h, s), right_part]
        to_left.append(copy_to(own, right, rs_.at[i], rr.at[i], leftward))
        to_above.append(copy_to(own, under, bs.at[i], br.at[i], above))
        on_above.append(copy_to(right, corner, ds.at[i], dr.at[i], above))
        on_sibling.append(copy_to(under, corner, ds.at[i], dr.at[i], leftward))
        if i >= half:
            a, b = i - half, i
            round_above.append(copy_to(own, via.at[a], bs.at[i], vr.at[a], detour))
            round_on.append(copy_to(right, via.at[b], ds.at[i], vr.at[b], detour))
            pass_above.append(copy_to(via.at[a], under, fs.at[a], br.at[i], onward))
            pass_on.append(copy_to(via.at[b], corner, fs.at[b], dr.at[i], onward))

    def upward(direct, rounds, i):
        if i < half:
            pl.when(r > 0)(direct[i].start)
        else:
            pl.when((r > 0) & (x > 0))(direct[i].start)
            pl.when(detours)(rounds[i - half].start)

    for i in range(len(cut)):
        to_left[i].start()
    for i in range(len(cut)):
        upward(to_above, round_above, i)
    region[:, :n, :n] = t[...]

    @pl.when(r == last_row)
    def _():
        region[:, n:, :] = jnp.zeros((2, n, 2 * n), F32)

    def pass_first():
        for a in range(half):
            round_above[a].wait_recv()
            pass_above[a].start()

    @pl.when(k == 1)
    def _():
        for i in range(len(cut)):
            @pl.when(r < last_row)
            def _():
                to_above[i].wait_recv()
                on_sibling[i].start()

            to_left[i].wait_recv()
            upward(on_above, round_on, i)
            if i == half - 1:
                pl.when(passes)(pass_first)

        @pl.when(passes)
        def _():
            for a in range(half):
                round_on[a].wait_recv()
                pass_on[a].start()

        for i in range(len(cut)):
            @pl.when(r < last_row)
            def _():
                on_above[i].wait_recv()
                on_sibling[i].wait_send()

            @pl.when(r > 0)
            def _():
                on_above[i].wait_send()

        @pl.when(passes)
        def _():
            for a in range(half):
                pass_on[a].wait_send()

    @pl.when(k == 0)
    def _():
        pl.when(passes)(pass_first)
        for i in range(len(cut)):
            to_left[i].wait_recv()

            @pl.when(r < last_row)
            def _():
                to_above[i].wait_recv()
                on_sibling[i].wait_recv()

    for i in range(len(cut)):
        to_left[i].wait_send()
        pl.when(r > 0)(to_above[i].wait_send)

    @pl.when(passes)
    def _():
        for a in range(half):
            pass_above[a].wait_send()

    @pl.when(c == last_col)
    def _():
        region[:, :, n:] = jnp.zeros((2, 2 * n, n), F32)


def gather_region(tile):
    n = tile.shape[-1]
    vm = pl.BlockSpec(memory_space=pltpu.VMEM)
    return pl.pallas_call(
        gather_kernel,
        out_shape=jax.ShapeDtypeStruct((2, 2 * n, 2 * n), F32),
        in_specs=[vm],
        out_specs=vm,
        scratch_shapes=[pltpu.VMEM((2 * CUTS, n // CUTS, n), F32)] + [pltpu.SemaphoreType.DMA((2 * CUTS,))] * 8,
        compiler_params=pltpu.CompilerParams(
            collective_id=1, has_side_effects=True, vmem_limit_bytes=12 * 1024 * 1024
        ),
    )(tile)


def on_device(transmission, probe_modes, measured, offset_down, offset_across):
    region = gather_region(transmission)
    scans = measured.shape[0] * lax.axis_size("row") * lax.axis_size("col")
    return gradients(offset_down, offset_across, region, probe_modes, measured, 1.0 / math.sqrt(scans))


def solution(mesh):
    in_specs = (
        P(None, "row", "col"),
        P(),
        P(("row", "col"), None, None),
        P(("row", "col")),
        P(("row", "col")),
    )
    out_specs = (P(None, "row", "col"), P())
    return jax.shard_map(
        on_device, mesh=mesh, in_specs=in_specs, out_specs=out_specs, check_vma=False
    )
```

```python
import functools
import math
import numpy as np
import jax
import jax.numpy as jnp
from jax import lax
from jax.experimental import pallas as pl
from jax.experimental.pallas import tpu as pltpu
from jax.sharding import PartitionSpec as P

F32, BF16 = jnp.float32, jnp.bfloat16


def split(v):
    high = v.astype(BF16)
    return high, (v - high.astype(F32)).astype(BF16)


def dft_tables(n):
    counter = np.arange(n)
    angles = (counter[:, None] * counter[None, :] % n) * (2.0 * math.pi / n)
    out = []
    for t in (np.cos(angles), np.sin(angles)):
        t = jnp.asarray((t / math.sqrt(n)).astype(np.float32))
        out += list(split(t))
    return jnp.stack(out)


def mm(a, b):
    return jnp.dot(a, b, preferred_element_type=F32)


def transform(c, s, pairs, sign):
    ch, cl = c
    sh, sl = s
    tc = [ch, ch, cl]
    ts = [sh, sh, sl]
    neg = [-sh, -sh, -sl]
    a, b = (neg, ts) if sign > 0 else (ts, neg)
    n = ch.shape[0]
    rows = jnp.concatenate([jnp.concatenate(tc + a, axis=1), jnp.concatenate(b + tc, axis=1)], axis=0)
    cols = jnp.concatenate([jnp.concatenate(tc + a, axis=0), jnp.concatenate(b + tc, axis=0)], axis=1)
    mid = []
    for re, im in pairs:
        r, i = split(re), split(im)
        v = mm(rows, jnp.concatenate([r[0], r[1], r[0], i[0], i[1], i[0]], axis=0))
        r, i = split(v[:n]), split(v[n:])
        mid.append(jnp.concatenate([r[0], r[1], r[0], i[0], i[1], i[0]], axis=1))
    v = mm(jnp.concatenate(mid, axis=0), cols)
    return [(v[j * n : (j + 1) * n, :n], v[j * n : (j + 1) * n, n:]) for j in range(len(pairs))]


MESH = pl.DeviceIdType.MESH
NX_, NYL, NYH, NZ, NK = 4, 4, 2, 12, 2
NY_ = NYL * NYH
CUTS = 4


def place():
    r, c = lax.axis_index("row"), lax.axis_index("col")
    y = lax.rem(lax.div(c, NK), NYH) * NYL + lax.div(r, NX_)
    return lax.rem(r, NX_), y, lax.div(c, NK * NYH), lax.rem(c, NK)


def device(x, y, z, k):
    row = lax.rem(y, NYL) * NX_ + x
    return {"row": row, "col": z * (NK * NYH) + lax.div(y, NYL) * NK + k}


def up(i, d, n):
    return lax.rem(i + d, n)


def send(src, dst, ss, rs, to):
    copy = copy_to(src, dst, ss, rs, to)
    copy.start()
    return copy


def shift_table(offset, wide, n):
    rows = lax.broadcasted_iota(jnp.int32, (wide, n), 0)
    cols = lax.broadcasted_iota(jnp.int32, (wide, n), 1)
    return jnp.where(rows == cols + offset, 1.0, 0.0).astype(BF16)


def select_table(offset, n, wide):
    rows = lax.broadcasted_iota(jnp.int32, (n, wide), 0)
    cols = lax.broadcasted_iota(jnp.int32, (n, wide), 1)
    return jnp.where(cols == rows + offset, 1.0, 0.0).astype(BF16)


def patch_of(high, low, y, x, n):
    rows = select_table(y, n, 2 * n)
    cols = shift_table(x, 2 * n, n)
    out = []
    for part in range(2):
        h = mm(rows, high[part]).astype(BF16)
        l = mm(rows, low[part]).astype(BF16)
        out.append(mm(h, cols) + mm(l, cols))
    return out


def place_terms(terms, ys, xs, n):
    scans = len(ys)
    rows = jnp.concatenate([shift_table(y, 2 * n, n) for y in ys] * 2, axis=1)
    cols = [select_table(x, n, 2 * n) for x in xs]
    out = []
    for part in range(2):
        high, low = [], []
        for scan in range(scans):
            h, l = split(terms[scan][part])
            high.append(mm(h, cols[scan]).astype(BF16))
            low.append(mm(l, cols[scan]).astype(BF16))
        out.append(mm(rows, jnp.concatenate(high + low, axis=0)))
    return out


class ProbeSum:
    def __init__(self, p, out, base, rows, where, bufs, sems, scale):
        self.p, self.out, self.base, self.scale = p, out, base, scale
        self.x, self.y, self.z, self.k = self.where = where
        self.half = rows // NK
        self.xb = self.half // NX_
        self.yb = self.xb // NY_
        self.cin, self.acc, self.xin, self.ysum, self.yin, self.zin = bufs
        self.sems = sems
        x, y, z, k = where
        self.sibling = device(x, y, z, 1 - k)
        self.xpeer = [device(up(x, d, NX_), y, z, k) for d in range(1, NX_)]
        self.ypeer = [device(x, up(y, d, NY_), z, k) for d in range(1, NY_)]
        self.zpeer = [device(x, y, up(z, d, NZ), k) for d in range(1, NZ)]
        self.order = [up(x, d, NX_) for d in range(1, NX_ + 1)]
        self.own = base + k * self.half + x * self.xb + y * self.yb

    def rows(self, start, size):
        return pl.ds(pl.multiple_of(start, 8), size)

    def start(self):
        s, r = self.sems[0]
        other = self.base + (1 - self.k) * self.half
        self.core = [
            send(self.p.at[self.rows(other + j * self.xb, self.xb)], self.cin.at[self.rows(j * self.xb, self.xb)], s.at[d], r.at[d], self.sibling)
            for d, j in enumerate(self.order)
        ]

    def along_x(self):
        s, r = self.sems[1]
        self.xc = []
        for d, j in enumerate(self.order):
            self.core[d].wait_recv()
            rows = self.rows(j * self.xb, self.xb)
            self.acc[rows] = self.p[self.rows(self.base + self.k * self.half + j * self.xb, self.xb)] + self.cin[rows]
            if d < NX_ - 1:
                self.xc.append(send(self.acc.at[rows], self.xin.at[d], s.at[d], r.at[d], self.xpeer[d]))

    def along_y(self):
        s, r = self.sems[2]
        for copy in self.xc:
            copy.wait_recv()
        self.yc = []
        for d in range(1, NY_ + 1):
            j = up(self.y, d, NY_)
            rows = self.rows(j * self.yb, self.yb)
            v = self.acc[self.rows(self.x * self.xb + j * self.yb, self.yb)]
            for i in range(NX_ - 1):
                v += self.xin[i, rows]
            self.ysum[rows] = v
            if d < NY_:
                self.yc.append(send(self.ysum.at[rows], self.yin.at[d - 1], s.at[d - 1], r.at[d - 1], self.ypeer[d - 1]))

    def along_z(self):
        s, r = self.sems[3]
        v = self.ysum[self.rows(self.y * self.yb, self.yb)]
        for i, copy in enumerate(self.yc):
            copy.wait_recv()
            v += self.yin[i]
        self.zin[self.z] = v
        self.zc = [send(self.zin.at[self.z], self.zin.at[self.z], s.at[d], r.at[d], self.zpeer[d]) for d in range(NZ - 1)]

    def to_sibling(self, e, rows):
        s, r = self.sems[6]
        self.cg.append(send(self.out.at[rows], self.out.at[rows], s.at[e], r.at[e], self.sibling))

    def back_y(self):
        s, r = self.sems[4]
        for copy in self.zc:
            copy.wait_recv()
        v = self.zin[0]
        for i in range(1, NZ):
            v += self.zin[i]
        own = self.rows(self.own, self.yb)
        self.out[own] = v * self.scale
        self.yg = [send(self.out.at[own], self.out.at[own], s.at[d], r.at[d], self.ypeer[d]) for d in range(NY_ - 1)]
        self.cg = []

    def back_x(self):
        s, r = self.sems[5]
        for copy in self.yg:
            copy.wait_recv()
        rows = self.rows(self.base + self.k * self.half + self.x * self.xb, self.xb)
        self.xg = [send(self.out.at[rows], self.out.at[rows], s.at[d], r.at[d], self.xpeer[d]) for d in range(NX_ - 1)]
        self.to_sibling(0, rows)

    def back_core(self):
        line = self.base + self.k * self.half
        for d in range(NX_ - 1):
            self.xg[d].wait_recv()
            self.to_sibling(d + 1, self.rows(line + up(self.x, NX_ - 1 - d, NX_) * self.xb, self.xb))

    def finish(self):
        for copy in self.cg:
            copy.wait_recv()
        for copy in self.core + self.xc + self.yc + self.zc + self.yg + self.xg + self.cg:
            copy.wait_send()


def gradients_kernel(scale, down, across, region, probe, measured, tables, tile, out, spread, patches, wave, terms, p,
                     left_in, above_in, side_in, corner_in, under_sum, right_sum, via, cin, acc, xin, ysum, yin, zin,
                     ls, lr, as_, ar, ss, sr, ks, kr, vr, fs, *sums):
    n = probe.shape[-1]
    modes, scans = probe.shape[0], measured.shape[0]
    r, c = lax.axis_index("row"), lax.axis_index("col")
    last_row = NX_ * NYL - 1
    x, y, z, k = place()
    per_mode = 2 * n
    probe_sums = [
        ProbeSum(p, out, m * per_mode, per_mode, (x, y, z, k), [v.at[m] for v in (cin, acc, xin, ysum, yin, zin)],
                 [(sums[2 * i].at[m], sums[2 * i + 1].at[m]) for i in range(len(sums) // 2)], scale)
        for m in range(modes)
    ]
    first, second = probe_sums
    sibling, xpeer, ypeer, zpeer = first.sibling, first.xpeer, first.ypeer, first.zpeer
    above, below, leftward, rightward = neighbours()
    y_lo = lax.div(r, NX_)
    detours = (x == NX_ - 1) & (r < last_row)
    passes = (x == 0) & (y_lo < NYL - 1)
    detour = {"row": lax.rem(r + NX_ * NYL - (NX_ - 1), NX_ * NYL), "col": c}
    onward = {"row": lax.rem(r + NX_, NX_ * NYL), "col": c}
    sources = [{"row": lax.rem(r + d, NX_ * NYL), "col": c} for d in (NX_ - 1, NX_ * NYL - NX_)]
    peers = [sibling, above, below, leftward, rightward] + sources + xpeer + ypeer + zpeer
    greet(peers)


    lo, hi = pl.ds(0, n), pl.ds(n, n)
    side_right = copy_to(spread.at[:, lo, hi], left_in, ls.at[0], lr.at[0], sibling)
    side_under = copy_to(spread.at[:, hi, hi], side_in, ss, sr, sibling)
    cut = pieces(n)
    middle = len(cut) // 2
    under, under_round, under_pass, corners, corner_round, corner_pass, rights, firsts = [[] for _ in range(8)]
    for i, (q, h, s) in enumerate(cut):
        rows = pl.ds(h, s)
        below_left, below_right = under_sum.at[q, rows], spread.at[q, pl.ds(n + h, s), hi]
        under.append(copy_to(below_left, above_in.at[q, rows], as_.at[i], ar.at[i], below))
        corners.append(copy_to(below_right, corner_in.at[q, rows], ks.at[i], kr.at[i], below))
        rights.append(copy_to(right_sum.at[q, rows], left_in.at[q, rows], ls.at[i], lr.at[i], rightward))
        firsts.append(copy_to(spread.at[q, rows, hi], left_in.at[q, rows], ls.at[i], lr.at[i], rightward))
        if i >= middle:
            e, f = i - middle, i
            under_round.append(copy_to(below_left, via.at[e], as_.at[i], vr.at[e], detour))
            corner_round.append(copy_to(below_right, via.at[f], ks.at[i], vr.at[f], detour))
            under_pass.append(copy_to(via.at[e], above_in.at[q, rows], fs.at[e], ar.at[i], onward))
            corner_pass.append(copy_to(via.at[f], corner_in.at[q, rows], fs.at[f], kr.at[i], onward))

    def downward(direct, rounds):
        for i in list(range(middle, len(cut))) + list(range(middle)):
            if i < middle:
                pl.when(r < last_row)(direct[i].start)
            else:
                pl.when((r < last_row) & (x < NX_ - 1))(direct[i].start)
                pl.when(detours)(rounds[i - middle].start)

    def pass_down(rounds, passing):
        @pl.when(passes)
        def _():
            for e in range(middle):
                rounds[e].wait_recv()
                passing[e].start()

    c_table, s_table = (tables[0], tables[1]), (tables[2], tables[3])
    ys = [down[scan] for scan in range(scans)]
    xs = [across[scan] for scan in range(scans)]
    high, low = zip(*[split(region[part]) for part in range(2)])
    for scan in range(scans):
        pr, pi = patch_of(high, low, ys[scan], xs[scan], n)
        patches[scan, 0], patches[scan, 1] = pr, pi
        exits = []
        for m in range(modes):
            mr, mi = probe[m, 0], probe[m, 1]
            exits.append((mr * pr - mi * pi, mr * pi + mi * pr))
        waves = transform(c_table, s_table, exits, -1.0)
        resid = -measured[scan]
        for wr, wi in waves:
            resid += wr * wr + wi * wi
        for m, (wr, wi) in enumerate(waves):
            wave[m, scan, 0], wave[m, scan, 1] = resid * wr, resid * wi
    for m in range(modes):
        backs = transform(c_table, s_table, [(wave[m, scan, 0], wave[m, scan, 1]) for scan in range(scans)], 1.0)
        mr, mi = probe[m, 0], probe[m, 1]
        qr = qi = 0.0
        for scan, (br, bi) in enumerate(backs):
            tr, ti = mr * br + mi * bi, mr * bi - mi * br
            if m == 0:
                terms[scan, 0], terms[scan, 1] = tr, ti
            else:
                terms[scan, 0] += tr
                terms[scan, 1] += ti
            pr, pi = patches[scan, 0], patches[scan, 1]
            qr += pr * br + pi * bi
            qi += pr * bi - pi * br
        p[m * per_mode : m * per_mode + n, :] = qr
        p[m * per_mode + n : (m + 1) * per_mode, :] = qi
        if m == 0:
            meet(peers)
        probe_sums[m].start()
        if m == 1:
            first.along_x()
    placed = place_terms([(terms[scan, 0], terms[scan, 1]) for scan in range(scans)], ys, xs, n)
    for part in range(2):
        spread[part] = placed[part]

    @pl.when(k == 0)
    def _():
        side_under.start()
        side_right.start()

    @pl.when(k == 1)
    def _():
        downward(corners, corner_round)

    @pl.when((k == 1) & (r == 0))
    def _():
        for copy in firsts:
            copy.start()

    second.along_x()
    first.along_y()

    @pl.when(k == 0)
    def _():
        under_sum[...] = spread[:, n:, :n]

    @pl.when(k == 1)
    def _():
        side_under.wait_recv()
        under_sum[...] = spread[:, n:, :n] + side_in[...]

    first.along_z()
    second.along_y()
    downward(under, under_round)

    @pl.when(k == 1)
    def _():
        pass_down(corner_round, corner_pass)

    @pl.when((k == 1) & (r > 0))
    def _():
        for i, (q, h, s) in enumerate(cut):
            corners[i].wait_recv()
            right_sum[q, h : h + s] = spread[q, h : h + s, n:] + corner_in[q, h : h + s]
            rights[i].start()

    second.along_z()
    pass_down(under_round, under_pass)
    first.back_y()
    second.back_y()
    first.back_x()
    second.back_x()

    first.back_core()
    second.back_core()

    @pl.when(r > 0)
    def _():
        for copy in under:
            copy.wait_recv()
        tile[...] = spread[:, :n, :n] + above_in[...]

    @pl.when(r == 0)
    def _():
        tile[...] = spread[:, :n, :n]

    @pl.when(k == 1)
    def _():
        side_right.wait_recv()

    @pl.when(k == 0)
    def _():
        for copy in rights:
            copy.wait_recv()

    @pl.when(c > 0)
    def _():
        tile[...] += left_in[...]

    first.finish()
    second.finish()

    @pl.when(k == 0)
    def _():
        side_under.wait_send()
        side_right.wait_send()

    @pl.when(k == 1)
    def _():
        for copy in rights:
            copy.wait_send()

    @pl.when(passes)
    def _():
        for copy in under_pass:
            copy.wait_send()

        @pl.when(k == 1)
        def _():
            for copy in corner_pass:
                copy.wait_send()

    @pl.when(r < last_row)
    def _():
        for copy in under:
            copy.wait_send()

        @pl.when(k == 1)
        def _():
            for copy in corners:
                copy.wait_send()


def gradients(down, across, region, probe, measured, scale):
    modes, _, n, _ = probe.shape
    scans = measured.shape[0]
    half = 2 * n // NK
    xb = half // NX_
    yb = xb // NY_
    dma = pltpu.SemaphoreType.DMA
    pairs = [(2 * CUTS,), (2 * CUTS,), (), (2 * CUTS,), (2 * CUTS,)]
    pairs += [(modes, *s) for s in ((NX_,), (NX_ - 1,), (NY_ - 1,), (NZ - 1,), (NY_ - 1,), (NX_ - 1,), (NX_,))]
    vm = pl.BlockSpec(memory_space=pltpu.VMEM)
    sm = pl.BlockSpec(memory_space=pltpu.SMEM)

    def f32(*shape):
        return pltpu.VMEM(shape, F32)

    tile, out = pl.pallas_call(
        functools.partial(gradients_kernel, scale),
        out_shape=[jax.ShapeDtypeStruct((2, n, n), F32), jax.ShapeDtypeStruct((modes * 2 * n, n), F32)],
        in_specs=[sm, sm, vm, vm, vm, vm],
        out_specs=[vm, vm],
        scratch_shapes=[
            f32(2, 2 * n, 2 * n),
            f32(scans, 2, n, n),
            f32(modes, scans, 2, n, n),
            f32(scans, 2, n, n),
            f32(modes * 2 * n, n),
        ]
        + [f32(2, n, n)] * 6
        + [
            f32(2 * CUTS, n // CUTS, n),
            f32(modes, half, n),
            f32(modes, half, n),
            f32(modes, NX_ - 1, xb, n),
            f32(modes, xb, n),
            f32(modes, NY_ - 1, yb, n),
            f32(modes, NZ, yb, n),
        ]
        + [dma(s) for s in pairs for _ in range(2)],
        compiler_params=pltpu.CompilerParams(
            collective_id=0, has_side_effects=True, vmem_limit_bytes=28 * 1024 * 1024
        ),
    )(down, across, region, probe, measured, dft_tables(n))
    return tile, out.reshape(probe.shape)


def neighbours():
    r, c = lax.axis_index("row"), lax.axis_index("col")
    rows, cols = NX_ * NYL, NZ * NYH * NK
    above = {"row": lax.rem(r + rows - 1, rows), "col": c}
    below = {"row": lax.rem(r + 1, rows), "col": c}
    leftward = {"row": r, "col": lax.rem(c + cols - 1, cols)}
    rightward = {"row": r, "col": lax.rem(c + 1, cols)}
    return above, below, leftward, rightward


def greet(peers):
    barrier = pltpu.get_barrier_semaphore()
    for peer in peers:
        pl.semaphore_signal(barrier, inc=1, device_id=peer, device_id_type=MESH)


def meet(peers):
    pl.semaphore_wait(pltpu.get_barrier_semaphore(), len(peers))


def copy_to(src, dst, ss, rs, to):
    return pltpu.make_async_remote_copy(
        src_ref=src, dst_ref=dst, send_sem=ss, recv_sem=rs, device_id=to, device_id_type=MESH
    )


def pieces(n):
    return [(part, h * (n // CUTS), n // CUTS) for part in range(2) for h in range(CUTS)]


def gather_kernel(t, region, via, rs_, rr, bs, br, ds, dr, vr, fs):
    n = t.shape[-1]
    r, c = lax.axis_index("row"), lax.axis_index("col")
    last_row, last_col = NX_ * NYL - 1, NZ * NYH * NK - 1
    k, x, y_lo = lax.rem(c, NK), lax.rem(r, NX_), lax.div(r, NX_)
    above, below, leftward, rightward = neighbours()
    detours = (x == 0) & (r > 0)
    passes = (x == NX_ - 1) & (y_lo > 0)
    detour = {"row": lax.rem(r + NX_ - 1, NX_ * NYL), "col": c}
    onward = {"row": lax.rem(r + NX_ * NYL - NX_, NX_ * NYL), "col": c}
    sources = [{"row": lax.rem(r + d, NX_ * NYL), "col": c} for d in (NX_ * NYL - NX_ + 1, NX_)]
    peers = [above, below, leftward, rightward] + sources
    greet(peers)
    meet(peers)

    left_part = pl.ds(0, n)
    right_part = pl.ds(n, n)
    cut = pieces(n)
    half = len(cut) // 2
    to_left, to_above, on_above, on_sibling = [], [], [], []
    round_above, round_on, pass_above, pass_on = [], [], [], []
    for i, (p, h, s) in enumerate(cut):
        own = t.at[p, pl.ds(h, s)]
        right = region.at[p, pl.ds(h, s), right_part]
        under = region.at[p, pl.ds(n + h, s), left_part]
        corner = region.at[p, pl.ds(n + h, s), right_part]
        to_left.append(copy_to(own, right, rs_.at[i], rr.at[i], leftward))
        to_above.append(copy_to(own, under, bs.at[i], br.at[i], above))
        on_above.append(copy_to(right, corner, ds.at[i], dr.at[i], above))
        on_sibling.append(copy_to(under, corner, ds.at[i], dr.at[i], leftward))
        if i >= half:
            a, b = i - half, i
            round_above.append(copy_to(own, via.at[a], bs.at[i], vr.at[a], detour))
            round_on.append(copy_to(right, via.at[b], ds.at[i], vr.at[b], detour))
            pass_above.append(copy_to(via.at[a], under, fs.at[a], br.at[i], onward))
            pass_on.append(copy_to(via.at[b], corner, fs.at[b], dr.at[i], onward))

    def upward(direct, rounds, i):
        if i < half:
            pl.when(r > 0)(direct[i].start)
        else:
            pl.when((r > 0) & (x > 0))(direct[i].start)
            pl.when(detours)(rounds[i - half].start)

    for i in range(len(cut)):
        to_left[i].start()

    @pl.when(x > 0)
    def _():
        for i in range(len(cut)):
            upward(to_above, round_above, i)

    region[:, :n, :n] = t[...]

    @pl.when(r == last_row)
    def _():
        region[:, n:, :] = jnp.zeros((2, n, 2 * n), F32)

    def pass_first():
        for a in range(half):
            round_above[a].wait_recv()
            pass_above[a].start()

    @pl.when(k == 1)
    def _():
        for i in range(len(cut)):
            to_left[i].wait_recv()

            @pl.when(x == 0)
            def _():
                upward(to_above, round_above, i)

            upward(on_above, round_on, i)
        pl.when(passes)(pass_first)

        @pl.when(r < last_row)
        def _():
            for i in range(len(cut)):
                to_above[i].wait_recv()
                on_sibling[i].start()

        @pl.when(passes)
        def _():
            for a in range(half):
                round_on[a].wait_recv()
                pass_on[a].start()

        for i in range(len(cut)):
            @pl.when(r < last_row)
            def _():
                on_above[i].wait_recv()
                on_sibling[i].wait_send()

            @pl.when(r > 0)
            def _():
                on_above[i].wait_send()

        @pl.when(passes)
        def _():
            for a in range(half):
                pass_on[a].wait_send()

    @pl.when(k == 0)
    def _():
        @pl.when(x == 0)
        def _():
            for i in range(len(cut)):
                to_left[i].wait_send()
                upward(to_above, round_above, i)

        pl.when(passes)(pass_first)
        for i in range(len(cut)):
            to_left[i].wait_recv()

            @pl.when(r < last_row)
            def _():
                to_above[i].wait_recv()
                on_sibling[i].wait_recv()

    for i in range(len(cut)):
        pl.when((x > 0) | (k == 1))(to_left[i].wait_send)
        pl.when(r > 0)(to_above[i].wait_send)

    @pl.when(passes)
    def _():
        for a in range(half):
            pass_above[a].wait_send()

    @pl.when(c == last_col)
    def _():
        region[:, :, n:] = jnp.zeros((2, 2 * n, n), F32)


def gather_region(tile):
    n = tile.shape[-1]
    vm = pl.BlockSpec(memory_space=pltpu.VMEM)
    return pl.pallas_call(
        gather_kernel,
        out_shape=jax.ShapeDtypeStruct((2, 2 * n, 2 * n), F32),
        in_specs=[vm],
        out_specs=vm,
        scratch_shapes=[pltpu.VMEM((2 * CUTS, n // CUTS, n), F32)] + [pltpu.SemaphoreType.DMA((2 * CUTS,))] * 8,
        compiler_params=pltpu.CompilerParams(
            collective_id=1, has_side_effects=True, vmem_limit_bytes=12 * 1024 * 1024
        ),
    )(tile)


def on_device(transmission, probe_modes, measured, offset_down, offset_across):
    region = gather_region(transmission)
    scans = measured.shape[0] * lax.axis_size("row") * lax.axis_size("col")
    return gradients(offset_down, offset_across, region, probe_modes, measured, 1.0 / math.sqrt(scans))


def solution(mesh):
    in_specs = (
        P(None, "row", "col"),
        P(),
        P(("row", "col"), None, None),
        P(("row", "col")),
        P(("row", "col")),
    )
    out_specs = (P(None, "row", "col"), P())
    return jax.shard_map(
        on_device, mesh=mesh, in_specs=in_specs, out_specs=out_specs, check_vma=False
    )
```
